256 devices in a mesh: lvl: 16 (over z, core), lat: 4 (over x), lon: 4 (over y).
Axes of the slice: x: 4, y: 4, z: 8, core: 2. Of those that a mesh axis runs over, the one named last changes fastest.
Arguments:
- patches: bfloat16 [16, 16, 24, 48, 1000], P('lvl', None, 'lat', 'lon'), may hold values from -6 to 6
- level_embed: float32 [16, 512], P('lvl'), may hold values from -6 to 6
- embed_weight: bfloat16 [1000, 512], replicated, may hold values from -0.1875 to 0.1875
- block_ids: int32 [16, 16, 4, 4, 3], P('lvl', None, 'lat', 'lon'), may hold values from -1 to 5, as said below
- latent_queries: bfloat16 [4, 512], replicated, may hold values from -6 to 6
- cross_gain: float32 [512], replicated, may hold values from 0.1 to 1.9
- cross_query: bfloat16 [512, 512], replicated, may hold values from -0.25 to 0.25
- cross_kv: bfloat16 [512, 1024], replicated, may hold values from -0.25 to 0.25
- cross_out: bfloat16 [512, 512], replicated, may hold values from -0.25 to 0.25
- region_ids: int32 [384, 48], P(('lvl', 'lat'), 'lon'), may hold values from 0 to 2
- swin_gain: float32 [512], replicated, may hold values from 0.1 to 1.9
- swin_qkv: bfloat16 [512, 1536], replicated, may hold values from -0.25 to 0.25
- swin_out: bfloat16 [512, 512], replicated, may hold values from -0.25 to 0.25
- mlp_gain: float32 [512], replicated, may hold values from 0.1 to 1.9
- mlp_up: bfloat16 [512, 2048], replicated, may hold values from -0.25 to 0.25
- mlp_down: bfloat16 [2048, 512], replicated, may hold values from -0.125 to 0.125
Outputs:
- latents: float32 [4, 384, 48, 512], P(None, ('lvl', 'lat'), 'lon')
The draws below stay inside these ranges and needn't reach their ends.
Inputs may be any that keep to these rules, and one draw needn't show every extreme that they name: block_ids[l, m, a, o, :] lists the column blocks b (longitude column (m * 4 + a) * 6 + b, latitude rows o * 12 to o * 12 + 11) at which level l is present: distinct numbers in its first slots, -1 in the remaining slots. Every column block is named by the list of at least one level. For every band and tile, the list of some level fills all 3 slots.
All inputs are finite; a program needn't handle non-finite values.
Results may differ from the reference program's by a relative error of at most 0.005.
Values may be sent and summed in bfloat16 or wider, within the bound.
No kernel may reach another device: no remote copies, remote signals or barrier semaphores. Data moves between devices by JAX's collectives and lax.ppermute only.
A program may use at most 64 MiB of HBM per device.

```python
import math
import jax
import jax.numpy as jnp
from jax import lax

D = 512
HEADS = 16
MLP = 2048
PF = 1000
LATENT = 4
WIN_LV = 2
WIN_LAT = 6
WIN_LON = 12
SH = 6
SW = 12
LEVELS = 16
BANDS = 16
LAT_TILES = 4
LON_TILES = 4
CAP = 3
NH = 384
NW = 48


def draw_block_ids(key, part):
    key_shuffle = jax.random.fold_in(key, 11)
    key_count = jax.random.fold_in(key, 12)
    key_full = jax.random.fold_in(key, 13)
    key_pick = jax.random.fold_in(key, 14)
    groups = (BANDS, LAT_TILES, LON_TILES)
    block_index = jnp.arange(SH, dtype=jnp.int32)
    shuffle = jax.random.randint(key_shuffle, groups + (SH,), 0, 1 << 20) * SH + block_index
    permuted = jnp.argsort(shuffle, axis=-1)
    position = jnp.argsort(permuted, axis=-1)
    duty_level = position % LEVELS
    level_index = jnp.arange(LEVELS, dtype=jnp.int32)
    required = (duty_level[None] == level_index[:, None, None, None, None]).astype(jnp.int32)
    need_count = jnp.sum(required, axis=-1)
    slot_count = jax.random.randint(key_count, need_count.shape, need_count, CAP + 1)
    full_level = jax.random.randint(key_full, groups, 0, LEVELS)
    slot_count = jnp.where(level_index[:, None, None, None] == full_level[None], CAP, slot_count)
    priority = jax.random.randint(key_pick, required.shape, 0, 1 << 20) * SH + block_index + required * (1 << 27)
    chosen = jnp.argsort(-priority, axis=-1)[..., :CAP].astype(jnp.int32)
    slot_index = jnp.arange(CAP, dtype=jnp.int32)
    return jnp.where(slot_index < slot_count[..., None], chosen, -1).astype(jnp.int32)


def plant(array, key, low, high):
    dims = array.shape
    place = [jax.random.randint(jax.random.fold_in(key, axis), (), 0, dims[axis]) for axis in range(len(dims))]
    array = array.at[tuple(place)].set(low)
    longest = dims.index(max(dims))
    place[longest] = (place[longest] + 1) % dims[longest]
    return array.at[tuple(place)].set(high)


def shard_levels(own_key, dims, cuts, smallest, high):
    loudness, own = 1.0, jax.random.fold_in(own_key, 6)
    for dim, blocks in cuts:
        draws = jnp.exp(jax.random.uniform(jax.random.fold_in(own, dim), (blocks,), jnp.float32, smallest / len(cuts), high / len(cuts)))
        loudness = loudness * jnp.repeat(draws, dims[dim] // blocks).reshape([-1 if axis == dim else 1 for axis in range(len(dims))])
    return loudness


def scatter_about(stream_key, dims, width, reach, split=(), kind=jnp.bfloat16):
    gain = shard_levels(stream_key, dims, split, -0.22, 0.18) if split else 1.0
    values = jax.random.normal(stream_key, dims, jnp.float32) * width * gain
    return jnp.minimum(jnp.maximum(values, -reach), reach).astype(kind)


def setup_inputs(seed: int = 0) -> dict:
    splits = jax.random.split(jax.random.key(seed), 17)
    return {
        "patches": scatter_about(splits[0], (LEVELS, BANDS, LAT_TILES * SH, NW, PF), 1.0, 6.0, ((0, 16), (2, 4), (3, 4))),
        "level_embed": scatter_about(splits[1], (LEVELS, D), 1.0, 6.0, ((0, 16),), jnp.float32),
        "embed_weight": scatter_about(splits[2], (PF, D), PF ** -0.5, 0.1875),
        "block_ids": draw_block_ids(jax.random.fold_in(splits[16], 71), 0),
        "latent_queries": scatter_about(splits[4], (LATENT, D), 1.0, 6.0),
        "cross_gain": jnp.clip(1.0 + 0.18 * jax.random.normal(splits[5], (D,), jnp.float32), 0.1, 1.9),
        "cross_query": scatter_about(splits[6], (D, D), D ** -0.5, 0.25),
        "cross_kv": scatter_about(splits[7], (D, 2 * D), D ** -0.5, 0.25),
        "cross_out": scatter_about(splits[8], (D, D), D ** -0.5, 0.25),
        "region_ids": plant(jax.random.randint(splits[9], (NH, NW), 0, 3), jax.random.fold_in(splits[9], 1), 0, 2).astype(jnp.int32),
        "swin_gain": jnp.clip(1.0 + 0.18 * jax.random.normal(splits[10], (D,), jnp.float32), 0.1, 1.9),
        "swin_qkv": scatter_about(splits[11], (D, 3 * D), D ** -0.5, 0.25),
        "swin_out": scatter_about(splits[12], (D, D), D ** -0.5, 0.25),
        "mlp_gain": jnp.clip(1.0 + 0.18 * jax.random.normal(splits[13], (D,), jnp.float32), 0.1, 1.9),
        "mlp_up": scatter_about(splits[14], (D, MLP), D ** -0.5, 0.25),
        "mlp_down": scatter_about(splits[15], (MLP, D), MLP ** -0.5, 0.125),
    }


def layer_norm(tensor, gain_vec):
    average = lax.optimization_barrier(jnp.mean(tensor, axis=-1, keepdims=True))
    centred = tensor - average
    spread = lax.optimization_barrier(jnp.mean(centred * centred, axis=-1, keepdims=True))
    return centred * lax.rsqrt(spread + 1e-05) * gain_vec

def to_windows(tensor, spans):
    trailing = tensor.shape[3:]
    level_span, row_span, col_span = tensor.shape[:3]
    first, second, third = spans
    shaped = tensor.reshape((level_span // first, first, row_span // second, second, col_span // third, third) + trailing)
    axes_order = (0, 2, 4, 1, 3, 5) + tuple(range(6, 6 + len(trailing)))
    return shaped.transpose(axes_order).reshape((level_span // first, row_span // second, col_span // third, first * second * third) + trailing)

def from_windows(tensor, extents, spans):
    trailing = tensor.shape[4:]
    level_span, row_span, col_span = extents
    first, second, third = spans
    shaped = tensor.reshape((level_span // first, row_span // second, col_span // third, first, second, third) + trailing)
    axes_order = (0, 3, 1, 4, 2, 5) + tuple(range(6, 6 + len(trailing)))
    return shaped.transpose(axes_order).reshape((level_span, row_span, col_span) + trailing)

def label_windows(labels, spans):
    row_span, col_span = labels.shape
    second, third = spans
    shaped = labels.reshape(row_span // second, second, col_span // third, third).transpose(0, 2, 1, 3)
    shaped = shaped.reshape(row_span // second, col_span // third, second * third)
    return jnp.concatenate([shaped] * WIN_LV, axis=-1)

def window_attend(queries, key_rows, value_rows, usable, labels):
    window_size = queries.shape[3]
    scores = jnp.einsum('abcqhe,abckhe->abchqk', queries.astype(jnp.float32), key_rows.astype(jnp.float32))
    same_label = labels[:, :, :, None] == labels[:, :, None, :]
    allowed = usable[:, :, :, None, None, :] & same_label[None, :, :, None, :, :]
    allowed = allowed | jnp.eye(window_size, dtype=jnp.bool_)
    exponent = jnp.where(allowed, jnp.exp(scores), jnp.zeros_like(scores))
    weights = (exponent / lax.optimization_barrier(jnp.sum(exponent, axis=-1, keepdims=True))).astype(jnp.bfloat16)
    mixture = jnp.einsum('abchqk,abckhe->abcqhe', weights.astype(jnp.float32), value_rows.astype(jnp.float32))
    return mixture.astype(jnp.bfloat16)

def reference(patches, level_embed, embed_weight, block_ids, latent_queries, cross_gain, cross_query, cross_kv, cross_out, region_ids, swin_gain, swin_qkv, swin_out, mlp_gain, mlp_up, mlp_down):
    head_dim = D // HEADS
    inv_root = 1.0 / math.sqrt(head_dim)
    band_rows = LAT_TILES * SH
    matches = jnp.any(block_ids[..., None] == jnp.arange(SH, dtype=jnp.int32), axis=4)
    matches = jnp.transpose(matches, (0, 1, 2, 4, 3)).reshape(LEVELS, BANDS, band_rows, LON_TILES)
    presence = jnp.repeat(matches.astype(jnp.float32), SW, axis=3)
    cross_queries = jnp.dot(latent_queries, cross_query, preferred_element_type=jnp.float32) * inv_root
    cross_queries = cross_queries.astype(jnp.bfloat16).reshape(LATENT, HEADS, head_dim)

    def one_band(inputs):
        band_patches, band_presence = inputs
        embedded = jnp.dot(band_patches.reshape(-1, PF), embed_weight, preferred_element_type=jnp.float32)
        embedded = embedded.reshape(LEVELS, band_rows, NW, D) + level_embed[:, None, None, :]
        embedded = embedded.astype(jnp.bfloat16)
        keys_in = layer_norm(embedded.astype(jnp.float32), cross_gain).astype(jnp.bfloat16)
        key_value = jnp.dot(keys_in.reshape(-1, D), cross_kv, preferred_element_type=jnp.float32).astype(jnp.bfloat16)
        key_value = key_value.reshape(LEVELS, band_rows, NW, 2, HEADS, head_dim)
        scores = jnp.einsum('qhe,lrche->qhlrc', cross_queries.astype(jnp.float32), key_value[:, :, :, 0].astype(jnp.float32))
        exponent = jnp.exp(scores) * band_presence[None, None]
        weights = (exponent / lax.optimization_barrier(jnp.sum(exponent, axis=2, keepdims=True))).astype(jnp.bfloat16)
        mixture = jnp.einsum('qhlrc,lrche->qrche', weights.astype(jnp.float32), key_value[:, :, :, 1].astype(jnp.float32))
        mixture = mixture.astype(jnp.bfloat16).reshape(-1, D)
        projected = jnp.dot(mixture, cross_out, preferred_element_type=jnp.float32).reshape(LATENT, band_rows, NW, D)
        return latent_queries.astype(jnp.float32)[:, None, None, :] + projected
    starts = lax.map(one_band, (jnp.moveaxis(patches, 1, 0), jnp.moveaxis(presence, 1, 0)))
    latent_start = jnp.moveaxis(starts, 0, 1).reshape(LATENT, NH, NW, D)
    normed = layer_norm(latent_start, swin_gain).astype(jnp.bfloat16)
    projected = jnp.dot(normed.reshape(-1, D), swin_qkv, preferred_element_type=jnp.float32)
    projected = projected.reshape(LATENT, NH, NW, 3, HEADS, head_dim)
    queries = (projected[:, :, :, 0] * inv_root).astype(jnp.bfloat16)
    key_rows = projected[:, :, :, 1].astype(jnp.bfloat16)
    value_rows = projected[:, :, :, 2].astype(jnp.bfloat16)
    level_pad = WIN_LV // 2
    col_margin = WIN_LAT // 2
    spans = (WIN_LV, WIN_LON, WIN_LAT)
    widths = ((level_pad, level_pad), (0, 0), (col_margin, col_margin), (0, 0), (0, 0))
    usable = jnp.pad(jnp.ones((LATENT, NH, NW), jnp.bool_), widths[:3])
    labels = jnp.pad(region_ids, ((0, 0), (col_margin, col_margin)))
    window_labels = label_windows(labels, (WIN_LON, WIN_LAT))
    inputs = (jnp.moveaxis(to_windows(jnp.pad(queries, widths), spans), 1, 0), jnp.moveaxis(to_windows(jnp.pad(key_rows, widths), spans), 1, 0), jnp.moveaxis(to_windows(jnp.pad(value_rows, widths), spans), 1, 0), jnp.moveaxis(to_windows(usable, spans), 1, 0), window_labels)

    def one_row(pieces):
        q_part, k_part, v_part, u_part, l_part = pieces
        return window_attend(q_part[:, None], k_part[:, None], v_part[:, None], u_part[:, None], l_part[None])[:, 0]
    mixture = jnp.moveaxis(lax.map(one_row, inputs), 0, 1)
    mixture = from_windows(mixture, (LATENT + 2 * level_pad, NH, NW + 2 * col_margin), spans)
    mixture = mixture[level_pad:level_pad + LATENT, :, col_margin:col_margin + NW]
    mixture = mixture.reshape(-1, D)
    attended = latent_start + jnp.dot(mixture, swin_out, preferred_element_type=jnp.float32).reshape(LATENT, NH, NW, D)
    mlp_in = layer_norm(attended, mlp_gain).astype(jnp.bfloat16).reshape(-1, D)
    hidden = jnp.dot(mlp_in, mlp_up, preferred_element_type=jnp.float32)
    activated = jax.nn.gelu(hidden, approximate=False).astype(jnp.bfloat16)
    lowered = jnp.dot(activated, mlp_down, preferred_element_type=jnp.float32).reshape(LATENT, NH, NW, D)
    return attended + lowered
```

```python
import functools
import math

import jax
import jax.numpy as jnp
import numpy as np
from jax import lax
from jax.experimental import pallas as pl
from jax.experimental.pallas import tpu as pltpu
from jax.sharding import PartitionSpec as P

D = 512
HEADS = 16
HEAD = D // HEADS
ROOT = 1.0 / math.sqrt(HEAD)
LEVELS = 16
LATENT = 4
CAP = 3
SH = 6
SW = 12
EDGE = 3
CELLS = SH * SW
UNIT = 72
TOKENS = LATENT * CELLS
SLOT_ROWS = 40
RECV = LEVELS * SLOT_ROWS
MESH_AXES = ("lvl", "lat", "lon")
NEG = -1e30
F32 = jnp.float32
BF16 = jnp.bfloat16


def unit_tokens(first_edge):
    order = []
    for levels in ((0, 3), (1, 2)):
        order += [(p, b, EDGE + j) for p in levels for b in range(SH) for j in range(2 * EDGE)]
    for start in (first_edge, SW - EDGE - first_edge):
        order += [(p, b, start + j) for p in range(LATENT) for b in range(SH) for j in range(EDGE)]
    return order


def permutations(first_edge):
    to_unit = np.zeros((TOKENS, TOKENS), np.float32)
    to_final = np.zeros((TOKENS, TOKENS), np.float32)
    for t, (p, b, j) in enumerate(unit_tokens(first_edge)):
        cell = b * SW + j
        to_unit[t, p * CELLS + cell] = 1
        to_final[cell * LATENT + p, t] = 1
    return to_unit, to_final


def final_permutation():
    out = np.zeros((TOKENS, TOKENS), np.float32)
    for cell in range(CELLS):
        for p in range(LATENT):
            out[cell * LATENT + p, p * CELLS + cell] = 1
    return out


def label_pickers():
    rows = np.zeros((3, 128, 128), np.float32)
    cols = np.zeros((2, 8, 128), np.float32)
    spans = np.zeros((8, 128), np.float32)
    tokens = unit_tokens(0)
    window = [(p + 1) // 2 for p in range(LATENT)]
    for i in range(UNIT):
        _, b, j = tokens[i]
        rows[0, j, i] = 1
        cols[0, b, i] = 1
        for u in range(3):
            spans[u, i] = 4 * window[tokens[u * UNIT + i][0]]
        _, b, j = tokens[2 * UNIT + i]
        rows[1, j, i] = 1
        rows[2, j + SW - EDGE, i] = 1
        cols[1, b, i] = 1
    return rows, cols, spans


def nt(a, b):
    return lax.dot_general(a, b, (((1,), (1,)), ((), ())), preferred_element_type=F32)


def mm(a, b):
    return jnp.dot(a, b, preferred_element_type=F32)


def norm(x, gain):
    mean = jnp.mean(x, axis=-1, keepdims=True)
    centred = x - mean
    var = jnp.mean(centred * centred, axis=-1, keepdims=True)
    return centred * lax.rsqrt(var + 1e-05) * gain


def head_rows():
    lane = lax.broadcasted_iota(jnp.int32, (HEADS, D), 1) // HEAD
    head = lax.broadcasted_iota(jnp.int32, (HEADS, D), 0)
    return jnp.where(lane == head, 1.0, 0.0).astype(F32)


def embed_kernel(ids, patches_hbm, weight_hbm, level, out, patches, weight, emb, sems):
    copy_w = pltpu.make_async_copy(weight_hbm, weight, sems.at[SH])
    copy_w.start()
    rows = SW * LEVELS
    copies = []
    for b in range(SH):
        part = pl.ds(b * rows, rows)
        copy = pltpu.make_async_copy(patches_hbm.at[part], patches.at[part], sems.at[b])
        copy.start()
        copies.append(copy)
    copy_w.wait()
    for b in range(SH):
        copies[b].wait()
        part = pl.ds(b * rows, rows)
        block = mm(patches[part, :], weight[...])
        for g in range(D // 128):
            emb[g, part, :] = block[:, g * 128 : (g + 1) * 128]
    shift = level[...]
    sub = lax.broadcasted_iota(jnp.int32, (SLOT_ROWS - CAP * SW, D), 0)
    for m in range(LEVELS):
        tail = jnp.full(sub.shape, -1.0, F32)
        parts = []
        for s in range(CAP):
            slot = ids[m, s]
            start = jnp.maximum(slot, 0) * rows + m
            picked = [emb[g, pl.ds(start, SW, stride=LEVELS), :] for g in range(D // 128)]
            parts.append(jnp.concatenate(picked, axis=1) + shift)
            tail = jnp.where(sub == s, slot.astype(F32), tail)
        out[m] = jnp.concatenate(parts + [tail], axis=0).astype(BF16)


def prep_kernel(own, other, far_a, far_b, pick_rows, pick_cols, spans, odd, lq, wq, wk,
                mid_bias, edge_bias, wkq):
    is_odd = odd[0] == 1
    high_first = jnp.where(is_odd, 1, 2)
    row_a = pick_rows[high_first]
    row_b = pick_rows[3 - high_first]

    def codes(labels, row_pick, which, span):
        spread = mm(labels, row_pick) * pick_cols[which]
        return jnp.sum(spread, axis=0, keepdims=True) + spans[span : span + 1, :]

    def column(row):
        return jnp.broadcast_to(row, (8, 128)).T[:UNIT, :1]

    def bias(query, keys):
        return jnp.concatenate(
            [jnp.where(column(query) == k[:, :UNIT], 0.0, NEG) for k in keys], axis=1
        )

    for g in range(2):
        mine = codes(own[...], pick_rows[0], 0, g)
        theirs = codes(other[...], pick_rows[0], 0, g)
        mid_bias[g] = bias(mine, [mine, theirs])
    for e, (near, away, far) in enumerate(((row_a, row_b, far_a), (row_b, row_a, far_b))):
        mine = codes(own[...], near, 1, 2)
        theirs = codes(other[...], near, 1, 2)
        halo = codes(far[0], away, 1, 2)
        halo_other = codes(far[1], away, 1, 2)
        edge_bias[e] = bias(mine, [mine, theirs, halo, halo_other])
    queries = (mm(lq[...], wq[...]) * ROOT).astype(BF16).astype(F32)
    mask = head_rows()
    masked = jnp.concatenate([queries[q : q + 1, :] * mask for q in range(LATENT)], axis=0)
    wkq[...] = nt(wk[...], masked.astype(BF16)).astype(BF16)


def cross_kernel(recv, gain, wkq, wv, lq, w_out, swin_gain, to_unit, normed, mixed):
    x = recv[...].astype(F32)
    keys_in = norm(x, gain[...]).astype(BF16)
    scores = mm(keys_in, wkq[...])
    values = mm(keys_in, wv[...]).astype(BF16).astype(F32)
    row = lax.broadcasted_iota(jnp.int32, (SLOT_ROWS, 128), 0)
    slot = jnp.where(row >= 2 * SW, 2, jnp.where(row >= SW, 1, 0))
    place = (row - slot * SW).astype(F32)
    real = row < CAP * SW
    tags = []
    for l in range(LEVELS):
        ids = x[l * SLOT_ROWS + 32 : (l + 1) * SLOT_ROWS, :128]
        block = jnp.where(slot == 0, ids[4:5], jnp.where(slot == 1, ids[5:6], ids[6:7]))
        tags.append(jnp.where(real & (block >= 0), block * SW + place, -1.0))
    tag = jnp.concatenate(tags, axis=0)
    lane = lax.broadcasted_iota(jnp.int32, (RECV, 128), 1).astype(F32)
    hit = jnp.where(tag == lane, 1.0, 0.0)
    hit_t = hit.T[:CELLS].astype(BF16)
    hit = hit.astype(BF16)
    present = tag[:, :64] >= 0
    weight = jnp.where(present, jnp.exp(scores), 0.0)

    def halves(v):
        high = v.astype(BF16)
        return jnp.concatenate([high.astype(F32), v - high.astype(F32)], axis=1).astype(BF16)

    total = mm(hit_t, halves(weight))
    total = total[:, :64] + total[:, 64:]
    spread = mm(hit[:, :CELLS], halves(total))
    spread = spread[:, :64] + spread[:, 64:]
    weight = (weight / jnp.where(present, spread, 1.0)).astype(BF16)
    mask = head_rows()
    starts = []
    for q in range(LATENT):
        pad = [jnp.zeros((HEADS, D), F32)] * LATENT
        pad[q] = mask
        wide = mm(weight, jnp.concatenate(pad, axis=0).astype(BF16))
        starts.append(mm(hit_t, (wide * values).astype(BF16)))
    mix = jnp.concatenate(starts, axis=0).astype(BF16)
    mixed[...] = mix
    projected = mm(mix, w_out[...])
    queries = lq[...].astype(F32)
    start = jnp.concatenate(
        [projected[q * CELLS : (q + 1) * CELLS] + queries[q : q + 1] for q in range(LATENT)], axis=0
    )
    unit = norm(start, swin_gain[...]).astype(BF16)
    normed[...] = mm(to_unit[...], unit).astype(BF16)


def own_kernel(normed, mixed, w_qkv, w_out, lq_rows, to_last, qkv, start):
    proj = mm(normed[...], w_qkv[...])
    qkv[:, :D] = proj[:, :D] * ROOT
    qkv[:, D:] = proj[:, D:]
    last = mm(to_last[...], mixed[...]).astype(BF16)
    start[...] = mm(last, w_out[...]) + lq_rows[...]


def attend(queries, keys, values, bias):
    rows = queries.shape[0]
    lane = lax.broadcasted_iota(jnp.int32, (rows, 128), 1) // HEAD
    masks = [jnp.where(lane == h, 1.0, 0.0) for h in range(4)]
    outs = []
    tall = jnp.concatenate([bias] * 4, axis=0)
    queries = queries.astype(BF16).astype(F32)
    for g in range(4):
        cols = slice(g * 128, (g + 1) * 128)
        stack = jnp.concatenate([queries[:, cols] * m for m in masks], axis=0).astype(BF16)
        scores = nt(stack, keys[:, cols]) + tall
        top = jnp.max(scores, axis=-1, keepdims=True)
        exps = jnp.exp(scores - top)
        total = jnp.sum(exps, axis=-1, keepdims=True)
        part = mm(exps.astype(BF16), values[:, cols]) / total
        out = part[:rows] * masks[0]
        for h in range(1, 4):
            out = out + part[h * rows : (h + 1) * rows] * masks[h]
        outs.append(out)
    return jnp.concatenate(outs, axis=1)


def mid_kernel(other, w_kv, qkv, bias, other_kv, mix):
    theirs = mm(other[...], w_kv[...])
    other_kv[...] = theirs[2 * UNIT :]
    for g in range(2):
        part = slice(g * UNIT, (g + 1) * UNIT)
        keys = jnp.concatenate([qkv[part, D : 2 * D], theirs[part, :D]], axis=0).astype(BF16)
        values = jnp.concatenate([qkv[part, 2 * D :], theirs[part, D:]], axis=0).astype(BF16)
        mix[part, :] = attend(qkv[part, :D], keys, values, bias[g])


def erf_gelu(v):
    return v * (1.0 + lax.erf(v * math.sqrt(0.5))) * 0.5


def last_kernel(halo_a, halo_b, w_kv, qkv, other_kv, bias, mid, w_out, start, to_final, mlp_gain,
                w_up, w_down, out):
    parts = [mid[...]]
    for e, halo in enumerate((halo_a, halo_b)):
        far = mm(halo[...], w_kv[...])
        own = slice((2 + e) * UNIT, (3 + e) * UNIT)
        theirs = slice(e * UNIT, (e + 1) * UNIT)
        keys = jnp.concatenate(
            [qkv[own, D : 2 * D], other_kv[theirs, :D], far[:, :D]], axis=0
        ).astype(BF16)
        values = jnp.concatenate(
            [qkv[own, 2 * D :], other_kv[theirs, D:], far[:, D:]], axis=0
        ).astype(BF16)
        parts.append(attend(qkv[own, :D], keys, values, bias[e]))
    mix = jnp.concatenate(parts, axis=0).astype(BF16)
    mix = mm(to_final[...], mix).astype(BF16)
    attended = start[...] + mm(mix, w_out[...])
    mlp_in = norm(attended, mlp_gain[...]).astype(BF16)
    total = attended
    width = w_up.shape[1]
    step = 512
    for c in range(0, width, step):
        hidden = erf_gelu(mm(mlp_in, w_up[:, c : c + step])).astype(BF16)
        total = total + mm(hidden, w_down[c : c + step, :])
    for b in range(SH):
        for j in range(SW):
            at = (b * SW + j) * LATENT
            out[b, j] = total[at : at + LATENT]


def call(kernel, outs, *args, smem=(), any_space=(), scratch=(), limit=48):
    specs = []
    for i in range(len(args)):
        space = pltpu.SMEM if i in smem else pl.ANY if i in any_space else pltpu.VMEM
        specs.append(pl.BlockSpec(memory_space=space))
    out_specs = [pl.BlockSpec(memory_space=pltpu.VMEM)] * len(outs)
    result = pl.pallas_call(
        kernel,
        out_shape=[jax.ShapeDtypeStruct(s, d) for s, d in outs],
        in_specs=specs,
        out_specs=out_specs,
        scratch_shapes=list(scratch),
        compiler_params=pltpu.CompilerParams(vmem_limit_bytes=limit << 20),
    )(*args)
    return result


def swap_pairs(change):
    pairs = []
    for l in range(LEVELS):
        for a in range(4):
            for o in range(4):
                target = change(a, o)
                if target is not None:
                    pairs.append(((l * 4 + a) * 4 + o, (l * 4 + target[0]) * 4 + target[1]))
    return pairs


def swap(block, pairs):
    return lax.ppermute(block, MESH_AXES, pairs)


def shards(patches, level_embed, embed_weight, block_ids, latent_queries, cross_gain, cross_query,
           cross_kv, cross_out, region_ids, swin_gain, swin_qkv, swin_out, mlp_gain, mlp_up, mlp_down):
    across = swap_pairs(lambda a, o: (a ^ 1, o))
    first = swap_pairs(lambda a, o: (a, o ^ 1))
    second = swap_pairs(lambda a, o: (a, 3 - o) if o in (1, 2) else None)
    odd = lax.axis_index("lon") % 2
    features = patches.shape[-1]

    flat = patches[0].transpose(1, 2, 0, 3).reshape(SH * SW * LEVELS, features)
    ids = block_ids.reshape(LEVELS, CAP)
    (packed,) = call(
        embed_kernel, [((LEVELS, SLOT_ROWS, D), BF16)], ids, flat, embed_weight, level_embed,
        smem=(0,), any_space=(1, 2),
        scratch=[
            pltpu.VMEM((SH * SW * LEVELS, features), BF16),
            pltpu.VMEM((features, D), BF16),
            pltpu.VMEM((D // 128, SH * SW * LEVELS, 128), F32),
            pltpu.SemaphoreType.DMA((SH + 1,)),
        ],
    )
    packed, region_ids, odd = lax.optimization_barrier((packed, region_ids, odd))
    received = lax.all_to_all(packed, "lvl", 0, 0, tiled=True).reshape(RECV, D)

    labels = jnp.pad(region_ids.astype(F32) + 1.0, ((0, 2), (0, 116)))
    other_labels = swap(labels, across)
    both = jnp.stack([labels, other_labels])
    far_a, far_b = swap(both, first), swap(both, second)
    rows, cols, spans = label_pickers()
    odd_one = odd.astype(jnp.int32).reshape(1)
    mid_bias, edge_bias, wkq = call(
        prep_kernel,
        [((2, UNIT, 2 * UNIT), F32), ((2, UNIT, 4 * UNIT), F32), ((D, LATENT * HEADS), BF16)],
        labels, other_labels, far_a, far_b, rows, cols, spans, odd_one, latent_queries, cross_query,
        cross_kv[:, :D], smem=(7,),
    )
    to_unit_even, to_final_even = permutations(SW - EDGE)
    to_unit_odd, to_final_odd = permutations(0)
    to_unit = jnp.where(odd == 1, to_unit_odd, to_unit_even).astype(BF16)
    to_final = jnp.where(odd == 1, to_final_odd, to_final_even).astype(BF16)
    to_last = jnp.asarray(final_permutation(), BF16)
    query_rows = jnp.tile(latent_queries.astype(F32), (CELLS, 1))

    normed, mixed = call(
        cross_kernel, [((TOKENS, D), BF16), ((TOKENS, D), BF16)],
        received, cross_gain[None], wkq, cross_kv[:, D:], latent_queries, cross_out, swin_gain[None],
        to_unit,
    )
    other = swap(normed, across)
    qkv, start = call(
        own_kernel, [((TOKENS, 3 * D), F32), ((TOKENS, D), F32)],
        normed, mixed, swin_qkv, cross_out, query_rows, to_last,
    )
    w_kv = swin_qkv[:, D:]
    edge_a = jnp.concatenate([normed[2 * UNIT : 3 * UNIT], other[2 * UNIT : 3 * UNIT]], axis=0)
    edge_b = jnp.concatenate([normed[3 * UNIT :], other[3 * UNIT :]], axis=0)
    halo_a, halo_b = swap(edge_a, first), swap(edge_b, second)
    other_kv, mid = call(
        mid_kernel, [((2 * UNIT, 2 * D), F32), ((2 * UNIT, D), F32)], other, w_kv, qkv, mid_bias
    )
    (out,) = call(
        last_kernel, [((SH, SW, LATENT, D), F32)],
        halo_a, halo_b, w_kv, qkv, other_kv, edge_bias, mid, swin_out, start, to_final,
        mlp_gain[None], mlp_up, mlp_down,
    )
    return out.transpose(2, 0, 1, 3)


def solution(mesh):
    return jax.shard_map(
        shards,
        mesh=mesh,
        in_specs=(
            P("lvl", None, "lat", "lon", None), P("lvl", None), P(), P("lvl", None, "lat", "lon", None),
            P(), P(), P(), P(), P(), P(("lvl", "lat"), "lon"), P(), P(), P(), P(), P(), P(),
        ),
        out_specs=P(None, ("lvl", "lat"), "lon", None),
        check_vma=False,
    )
```

```python
import functools
import math

import jax
import jax.numpy as jnp
import numpy as np
from jax import lax
from jax.experimental import pallas as pl
from jax.experimental.pallas import tpu as pltpu
from jax.sharding import PartitionSpec as P

D = 512
HEADS = 16
HEAD = D // HEADS
ROOT = 1.0 / math.sqrt(HEAD)
LEVELS = 16
LATENT = 4
CAP = 3
SH = 6
SW = 12
EDGE = 3
CELLS = SH * SW
UNIT = 72
HALF = 40
HALVES = ((0, HALF), (UNIT - HALF, UNIT))
TOKENS = LATENT * CELLS
SLOT_ROWS = 40
RECV = LEVELS * SLOT_ROWS
MESH_AXES = ("lvl", "lat", "lon")
NEG = -1e30
F32 = jnp.float32
BF16 = jnp.bfloat16


def unit_tokens(first_edge):
    order = []
    for levels in ((0, 3), (1, 2)):
        order += [(p, b, EDGE + j) for p in levels for b in range(SH) for j in range(2 * EDGE)]
    for start in (first_edge, SW - EDGE - first_edge):
        order += [(p, b, start + j) for p in (0, 3, 1, 2) for b in range(SH) for j in range(EDGE)]
    return order


def permutations(first_edge):
    to_unit = np.zeros((TOKENS, TOKENS), np.float32)
    to_final = np.zeros((TOKENS, TOKENS), np.float32)
    for t, (p, b, j) in enumerate(unit_tokens(first_edge)):
        cell = b * SW + j
        to_unit[t, p * CELLS + cell] = 1
        to_final[cell * LATENT + p, t] = 1
    return to_unit, to_final


def final_permutation():
    out = np.zeros((TOKENS, TOKENS), np.float32)
    for cell in range(CELLS):
        for p in range(LATENT):
            out[cell * LATENT + p, p * CELLS + cell] = 1
    return out


def label_pickers():
    rows = np.zeros((3, 128, 128), np.float32)
    cols = np.zeros((2, 8, 128), np.float32)
    spans = np.zeros((8, 128), np.float32)
    tokens = unit_tokens(0)
    window = [(p + 1) // 2 for p in range(LATENT)]
    for i in range(UNIT):
        _, b, j = tokens[i]
        rows[0, j, i] = 1
        cols[0, b, i] = 1
        for u in range(3):
            spans[u, i] = 4 * window[tokens[u * UNIT + i][0]]
        _, b, j = tokens[2 * UNIT + i]
        rows[1, j, i] = 1
        rows[2, j + SW - EDGE, i] = 1
        cols[1, b, i] = 1
    return rows, cols, spans


def nt(a, b):
    return lax.dot_general(a, b, (((1,), (1,)), ((), ())), preferred_element_type=F32)


def mm(a, b):
    return jnp.dot(a, b, preferred_element_type=F32)


def norm(x, gain):
    mean = jnp.mean(x, axis=-1, keepdims=True)
    centred = x - mean
    var = jnp.mean(centred * centred, axis=-1, keepdims=True)
    return centred * lax.rsqrt(var + 1e-05) * gain


def head_rows():
    lane = lax.broadcasted_iota(jnp.int32, (HEADS, D), 1) // HEAD
    head = lax.broadcasted_iota(jnp.int32, (HEADS, D), 0)
    return jnp.where(lane == head, 1.0, 0.0).astype(F32)


def embed_kernel(ids_hbm, patches_hbm, weight_hbm, level_hbm, out_hbm, patches, weight, level, emb,
                 packed, ids, sems):
    copy_ids = pltpu.make_async_copy(ids_hbm, ids, sems.at[SH + 2 + LEVELS])
    copy_ids.start()
    copy_w = pltpu.make_async_copy(weight_hbm, weight, sems.at[SH])
    copy_w.start()
    rows = SW * LEVELS
    copies = []
    for b in range(SH):
        part = pl.ds(b * rows, rows)
        copy = pltpu.make_async_copy(patches_hbm.at[part], patches.at[part], sems.at[b])
        copy.start()
        copies.append(copy)
    copy_level = pltpu.make_async_copy(level_hbm, level, sems.at[SH + 1])
    copy_level.start()
    copy_w.wait()
    for b in range(SH):
        copies[b].wait()
        part = pl.ds(b * rows, rows)
        block = mm(patches[part, :], weight[...])
        for g in range(D // 128):
            emb[g, part, :] = block[:, g * 128 : (g + 1) * 128]
    copy_level.wait()
    copy_ids.wait()
    shift = level[...]
    sub = lax.broadcasted_iota(jnp.int32, (SLOT_ROWS - CAP * SW, D), 0)
    sends = []
    for m in range(LEVELS):
        tail = jnp.full(sub.shape, -1.0, F32)
        parts = []
        for s in range(CAP):
            slot = ids[s, 0, m]
            start = jnp.maximum(slot, 0) * rows + m
            picked = [emb[g, pl.ds(start, SW, stride=LEVELS), :] for g in range(D // 128)]
            parts.append(jnp.concatenate(picked, axis=1) + shift)
            tail = jnp.where(sub == s, slot.astype(F32), tail)
        packed[m] = jnp.concatenate(parts + [tail], axis=0).astype(BF16)
        send = pltpu.make_async_copy(packed.at[m], out_hbm.at[m], sems.at[SH + 2 + m])
        send.start()
        sends.append(send)
    for send in sends:
        send.wait()


def prep_kernel(own, other, far_a, far_b, pick_rows, pick_cols, spans, odd, mid_bias, edge_bias):
    is_odd = odd[0] == 1
    high_first = jnp.where(is_odd, 1, 2)
    row_a = pick_rows[high_first]
    row_b = pick_rows[3 - high_first]

    def codes(labels, row_pick, which, span):
        spread = mm(labels, row_pick) * pick_cols[which]
        return jnp.sum(spread, axis=0, keepdims=True) + spans[span : span + 1, :]

    def column(row):
        return jnp.broadcast_to(row, (8, 128)).T[:UNIT, :1]

    def bias(query, keys):
        return jnp.concatenate(
            [jnp.where(column(query) == k[:, :UNIT], 0.0, NEG) for k in keys], axis=1
        )

    for g in range(2):
        mine = codes(own[...], pick_rows[0], 0, g)
        theirs = codes(other[...], pick_rows[0], 0, g)
        mid_bias[g] = bias(mine, [mine, theirs])
    for e, (near, away, far) in enumerate(((row_a, row_b, far_a), (row_b, row_a, far_b))):
        mine = codes(own[...], near, 1, 2)
        theirs = codes(other[...], near, 1, 2)
        halo = codes(far[0], away, 1, 2)
        halo_other = codes(far[1], away, 1, 2)
        for g, (low, high) in enumerate(HALVES):
            parts = [k[:, low:high] for k in (mine, theirs, halo, halo_other)]
            keys = jnp.concatenate(parts, axis=1)
            edge_bias[e, g] = jnp.where(column(mine)[low:high] == keys, 0.0, NEG)


def cross_kernel(recv, gain, wq, w_kv, lq, w_out, swin_gain, to_unit, normed, edges,
                 mixed_hbm, mixed, sem):
    queries = (mm(lq[...], wq[...]) * ROOT).astype(BF16).astype(F32)
    mask = head_rows()
    masked = jnp.concatenate([queries[q : q + 1, :] * mask for q in range(LATENT)], axis=0)
    wkq = nt(w_kv[:, :D], masked.astype(BF16)).astype(BF16)
    x = recv[...].astype(F32)
    keys_in = norm(x, gain[...]).astype(BF16)
    values = mm(keys_in, w_kv[:, D:]).astype(BF16).astype(F32)
    scores = mm(keys_in, wkq)
    row = lax.broadcasted_iota(jnp.int32, (SLOT_ROWS, 128), 0)
    slot = jnp.where(row >= 2 * SW, 2, jnp.where(row >= SW, 1, 0))
    place = (row - slot * SW).astype(F32)
    real = row < CAP * SW
    tags = []
    for l in range(LEVELS):
        ids = x[l * SLOT_ROWS + 32 : (l + 1) * SLOT_ROWS, :128]
        block = jnp.where(slot == 0, ids[4:5], jnp.where(slot == 1, ids[5:6], ids[6:7]))
        tags.append(jnp.where(real & (block >= 0), block * SW + place, -1.0))
    tag = jnp.concatenate(tags, axis=0)
    lane = lax.broadcasted_iota(jnp.int32, (RECV, 128), 1).astype(F32)
    hit = jnp.where(tag == lane, 1.0, 0.0)
    hit_t = hit.T[:CELLS].astype(BF16)
    hit = hit.astype(BF16)
    present = tag[:, :64] >= 0
    weight = jnp.where(present, jnp.exp(scores), 0.0)

    def halves(v):
        high = v.astype(BF16)
        return jnp.concatenate([high.astype(F32), v - high.astype(F32)], axis=1).astype(BF16)

    total = mm(hit_t, halves(weight))
    total = total[:, :64] + total[:, 64:]
    spread = mm(hit[:, :CELLS], halves(total))
    spread = spread[:, :64] + spread[:, 64:]
    weight = (weight / jnp.where(present, spread, 1.0)).astype(BF16)
    starts = []
    for q in range(LATENT):
        pad = [jnp.zeros((HEADS, D), F32)] * LATENT
        pad[q] = mask
        wide = mm(weight, jnp.concatenate(pad, axis=0).astype(BF16))
        starts.append(mm(hit_t, (wide * values).astype(BF16)))
    mix = jnp.concatenate(starts, axis=0).astype(BF16)
    mixed[...] = mix
    keep = pltpu.make_async_copy(mixed, mixed_hbm, sem)
    keep.start()
    projected = mm(mix, w_out[...])
    queries = lq[...].astype(F32)
    start = jnp.concatenate(
        [projected[q * CELLS : (q + 1) * CELLS] + queries[q : q + 1] for q in range(LATENT)], axis=0
    )
    unit = norm(start, swin_gain[...]).astype(BF16)
    placed = mm(to_unit[...], unit)
    normed[...] = placed.astype(BF16)
    edges[0] = placed[2 * UNIT : 3 * UNIT].astype(BF16)
    edges[1] = placed[3 * UNIT :].astype(BF16)
    keep.wait()


def own_kernel(normed, mixed, w_qkv, w_out, lq, to_last, qkv, start, centre):
    centre[...] = normed[: 2 * UNIT, :]
    proj = mm(normed[...], w_qkv[...])
    qkv[:, :D] = proj[:, :D] * ROOT
    qkv[:, D:] = proj[:, D:]
    last = mm(to_last[...], mixed[...]).astype(BF16)
    level = lax.broadcasted_iota(jnp.int32, (TOKENS, D), 0) % LATENT
    queries = lq[...].astype(F32)
    rows = jnp.broadcast_to(queries[LATENT - 1 :], (TOKENS, D))
    for p in range(LATENT - 1):
        rows = jnp.where(level == p, queries[p : p + 1], rows)
    start[...] = mm(last, w_out[...]) + rows


def attend(queries, keys, values, bias):
    rows = queries.shape[0]
    lane = lax.broadcasted_iota(jnp.int32, (rows, 128), 1) // HEAD
    masks = [jnp.where(lane == h, 1.0, 0.0) for h in range(4)]
    outs = []
    tall = jnp.concatenate([bias] * 4, axis=0)
    queries = queries.astype(BF16).astype(F32)
    for g in range(4):
        cols = slice(g * 128, (g + 1) * 128)
        stack = jnp.concatenate([queries[:, cols] * m for m in masks], axis=0).astype(BF16)
        scores = nt(stack, keys[:, cols]) + tall
        top = jnp.max(scores, axis=-1, keepdims=True)
        exps = jnp.exp(scores - top)
        total = jnp.sum(exps, axis=-1, keepdims=True)
        part = mm(exps.astype(BF16), values[:, cols]) / total
        out = part[:rows] * masks[0]
        for h in range(1, 4):
            out = out + part[h * rows : (h + 1) * rows] * masks[h]
        outs.append(out)
    return jnp.concatenate(outs, axis=1)


def pair_kernel(own, other, pair_a, pair_b):
    for e, pair in enumerate((pair_a, pair_b)):
        pair[0] = own[e]
        pair[1] = other[e]


def mid_kernel(other, other_edges, w_qkv, qkv, bias, other_kv, mix):
    for e in range(2):
        other_kv[e * UNIT : (e + 1) * UNIT, :] = mm(other_edges[e], w_qkv[:, D:])
    theirs = mm(other[...], w_qkv[:, D:])
    for g in range(2):
        part = slice(g * UNIT, (g + 1) * UNIT)
        keys = jnp.concatenate([qkv[part, D : 2 * D], theirs[part, :D]], axis=0).astype(BF16)
        values = jnp.concatenate([qkv[part, 2 * D :], theirs[part, D:]], axis=0).astype(BF16)
        mix[part, :] = attend(qkv[part, :D], keys, values, bias[g])


def erf_gelu(v):
    return v * (1.0 + lax.erf(v * math.sqrt(0.5))) * 0.5


def last_kernel(far_a, far_b, w_qkv, qkv, other_kv, bias, mid, w_out, start, to_final, mlp_gain,
                w_up, w_down, out):
    parts = [mid[...]]
    upper = lax.broadcasted_iota(jnp.int32, (2 * HALF - UNIT, D), 0) < UNIT // 2 - HALVES[1][0]
    for e, far in enumerate((far_a, far_b)):
        own = slice((2 + e) * UNIT, (3 + e) * UNIT)
        theirs = slice(e * UNIT, (e + 1) * UNIT)
        pieces = [qkv[own, D:], other_kv[theirs, :]]
        pieces += [mm(far[i], w_qkv[:, D:]) for i in range(2)]
        queries = qkv[own, :D]
        done = []
        for g, (low, high) in enumerate(HALVES):
            keys = jnp.concatenate([p[low:high, :D] for p in pieces], axis=0).astype(BF16)
            values = jnp.concatenate([p[low:high, D:] for p in pieces], axis=0).astype(BF16)
            done.append(attend(queries[low:high], keys, values, bias[e, g]))
        cut = HALVES[1][0]
        shared = jnp.where(upper, done[0][cut:], done[1][: HALF - cut])
        parts += [done[0][:cut], shared, done[1][HALF - cut :]]
    mix = jnp.concatenate(parts, axis=0).astype(BF16)
    mix = mm(to_final[...], mix).astype(BF16)
    attended = start[...] + mm(mix, w_out[...])
    mlp_in = norm(attended, mlp_gain[...]).astype(BF16)
    total = attended
    width = w_up.shape[1]
    step = 512
    for c in range(0, width, step):
        hidden = erf_gelu(mm(mlp_in, w_up[:, c : c + step])).astype(BF16)
        total = total + mm(hidden, w_down[c : c + step, :])
    for b in range(SH):
        for j in range(SW):
            at = (b * SW + j) * LATENT
            out[b, j] = total[at : at + LATENT]


def call(kernel, outs, *args, smem=(), hbm=(), hbm_out=(), scratch=(), limit=24, flops=10**9):
    specs = []
    for i in range(len(args)):
        space = pltpu.SMEM if i in smem else pltpu.HBM if i in hbm else pltpu.VMEM
        specs.append(pl.BlockSpec(memory_space=space))
    out_specs = [
        pl.BlockSpec(memory_space=pltpu.HBM if i in hbm_out else pltpu.VMEM) for i in range(len(outs))
    ]
    moved = sum(a.size * a.dtype.itemsize for a in args)
    return pl.pallas_call(
        kernel,
        out_shape=[jax.ShapeDtypeStruct(s, d) for s, d in outs],
        in_specs=specs,
        out_specs=out_specs,
        scratch_shapes=list(scratch),
        compiler_params=pltpu.CompilerParams(vmem_limit_bytes=limit << 20),
        cost_estimate=pl.CostEstimate(flops=flops, bytes_accessed=moved, transcendentals=0),
    )(*args)


def swap_pairs(change):
    pairs = []
    for l in range(LEVELS):
        for a in range(4):
            for o in range(4):
                target = change(a, o)
                if target is not None:
                    pairs.append(((l * 4 + a) * 4 + o, (l * 4 + target[0]) * 4 + target[1]))
    return pairs


def swap(block, pairs):
    return lax.ppermute(block, MESH_AXES, pairs)


def shards(patches, level_embed, embed_weight, block_ids, latent_queries, cross_gain, cross_query,
           cross_kv, cross_out, region_ids, swin_gain, swin_qkv, swin_out, mlp_gain, mlp_up, mlp_down):
    across = swap_pairs(lambda a, o: (a ^ 1, o))
    first = swap_pairs(lambda a, o: (a, o ^ 1))
    second = swap_pairs(lambda a, o: (a, 3 - o) if o in (1, 2) else None)
    odd = lax.axis_index("lon") % 2
    features = patches.shape[-1]

    flat = patches[0].transpose(1, 2, 0, 3).reshape(SH * SW * LEVELS, features)
    ids = block_ids.transpose(0, 2, 4, 3, 1).reshape(CAP, 1, LEVELS)
    (packed,) = call(
        embed_kernel, [((LEVELS, SLOT_ROWS, D), BF16)], ids, flat, embed_weight, level_embed,
        hbm=(0, 1, 2, 3), hbm_out=(0,), limit=63,
        scratch=[
            pltpu.VMEM((SH * SW * LEVELS, features), BF16),
            pltpu.VMEM((features, D), BF16),
            pltpu.VMEM((1, D), F32),
            pltpu.VMEM((D // 128, SH * SW * LEVELS, 128), F32),
            pltpu.VMEM((LEVELS, SLOT_ROWS, D), BF16),
            pltpu.SMEM((CAP, 1, LEVELS), jnp.int32),
            pltpu.SemaphoreType.DMA((SH + 3 + LEVELS,)),
        ],
    )
    packed, region_ids, odd = lax.optimization_barrier((packed, region_ids, odd))
    received = lax.all_to_all(packed, "lvl", 0, 0, tiled=True).reshape(RECV, D)

    labels = jnp.pad(region_ids.astype(F32) + 1.0, ((0, 2), (0, 116)))
    other_labels = swap(labels, across)
    both = jnp.stack([labels, other_labels])
    far_a, far_b = swap(both, first), swap(both, second)
    rows, cols, spans = label_pickers()
    odd_one = odd.astype(jnp.int32).reshape(1)
    mid_bias, edge_bias = call(
        prep_kernel, [((2, UNIT, 2 * UNIT), F32), ((2, 2, HALF, 4 * HALF), F32)],
        labels, other_labels, far_a, far_b, rows, cols, spans, odd_one, smem=(7,),
    )
    to_unit_even, to_final_even = permutations(SW - EDGE)
    to_unit_odd, to_final_odd = permutations(0)
    to_unit = jnp.where(odd == 1, to_unit_odd, to_unit_even).astype(BF16)
    to_final = jnp.where(odd == 1, to_final_odd, to_final_even).astype(BF16)
    to_last = jnp.asarray(final_permutation(), BF16)

    received, mid_bias, edge_bias = lax.optimization_barrier((received, mid_bias, edge_bias))
    normed, edges, mixed = call(
        cross_kernel, [((TOKENS, D), BF16), ((2, UNIT, D), BF16), ((TOKENS, D), BF16)],
        received, cross_gain[None], cross_query, cross_kv, latent_queries, cross_out, swin_gain[None],
        to_unit, hbm_out=(2,), flops=4 * 10**9,
        scratch=[pltpu.VMEM((TOKENS, D), BF16), pltpu.SemaphoreType.DMA],
    )
    other_edges = swap(edges, across)
    qkv, start, centre = call(
        own_kernel, [((TOKENS, 3 * D), F32), ((TOKENS, D), F32), ((2 * UNIT, D), BF16)],
        normed, mixed, swin_qkv, cross_out, latent_queries, to_last, flops=3 * 10**9,
    )
    other_centre = swap(centre, across)
    pair_a, pair_b = call(pair_kernel, [((2, UNIT, D), BF16)] * 2, edges, other_edges)
    halo_a, halo_b = swap(pair_a, first), swap(pair_b, second)
    other_kv, mid = call(
        mid_kernel, [((2 * UNIT, 2 * D), F32), ((2 * UNIT, D), F32)], other_centre, other_edges, swin_qkv, qkv, mid_bias,
        flops=3 * 10**9,
    )
    (out,) = call(
        last_kernel, [((SH, SW, LATENT, D), F32)],
        halo_a, halo_b, swin_qkv, qkv, other_kv, edge_bias, mid, swin_out, start, to_final,
        mlp_gain[None], mlp_up, mlp_down, flops=8 * 10**9,
    )
    return out.transpose(2, 0, 1, 3)


def solution(mesh):
    return jax.shard_map(
        shards,
        mesh=mesh,
        in_specs=(
            P("lvl", None, "lat", "lon", None), P("lvl", None), P(), P("lvl", None, "lat", "lon", None),
            P(), P(), P(), P(), P(), P(("lvl", "lat"), "lon"), P(), P(), P(), P(), P(), P(),
        ),
        out_specs=P(None, ("lvl", "lat"), "lon", None),
        check_vma=False,
    )
```

```python
import functools
import math

import jax
import jax.numpy as jnp
import numpy as np
from jax import lax
from jax.experimental import pallas as pl
from jax.experimental.pallas import tpu as pltpu
from jax.sharding import PartitionSpec as P

D = 512
HEADS = 16
HEAD = D // HEADS
ROOT = 1.0 / math.sqrt(HEAD)
LEVELS = 16
LATENT = 4
CAP = 3
SH = 6
SW = 12
EDGE = 3
CELLS = SH * SW
UNIT = 72
HALF = 40
HALVES = ((0, HALF), (UNIT - HALF, UNIT))
TOKENS = LATENT * CELLS
SLOT_ROWS = CAP * SW
MAIN = 32
REST = SLOT_ROWS - MAIN
GROUPS = D // 128
SENT = GROUPS * SLOT_ROWS + 8
RECV = LEVELS * SLOT_ROWS
MESH_AXES = ("lvl", "lat", "lon")
NEG = -1e30
F32 = jnp.float32
BF16 = jnp.bfloat16


def unit_tokens(first_edge):
    order = []
    for levels in ((0, 3), (1, 2)):
        order += [(p, b, EDGE + j) for p in levels for b in range(SH) for j in range(2 * EDGE)]
    for start in (first_edge, SW - EDGE - first_edge):
        order += [(p, b, start + j) for p in (0, 3, 1, 2) for b in range(SH) for j in range(EDGE)]
    return order


def permutations(first_edge):
    to_unit = np.zeros((TOKENS, TOKENS), np.float32)
    to_final = np.zeros((TOKENS, TOKENS), np.float32)
    for t, (p, b, j) in enumerate(unit_tokens(first_edge)):
        cell = b * SW + j
        to_unit[t, p * CELLS + cell] = 1
        to_final[cell * LATENT + p, t] = 1
    return to_unit, to_final


def final_permutation():
    out = np.zeros((TOKENS, TOKENS), np.float32)
    for cell in range(CELLS):
        for p in range(LATENT):
            out[cell * LATENT + p, p * CELLS + cell] = 1
    return out


def label_pickers():
    rows = np.zeros((3, 128, 128), np.float32)
    cols = np.zeros((2, 8, 128), np.float32)
    spans = np.zeros((8, 128), np.float32)
    tokens = unit_tokens(0)
    window = [(p + 1) // 2 for p in range(LATENT)]
    for i in range(UNIT):
        _, b, j = tokens[i]
        rows[0, j, i] = 1
        cols[0, b, i] = 1
        for u in range(3):
            spans[u, i] = 4 * window[tokens[u * UNIT + i][0]]
        _, b, j = tokens[2 * UNIT + i]
        rows[1, j, i] = 1
        rows[2, j + SW - EDGE, i] = 1
        cols[1, b, i] = 1
    return rows, cols, spans


def nt(a, b):
    return lax.dot_general(a, b, (((1,), (1,)), ((), ())), preferred_element_type=F32)


def mm(a, b):
    return jnp.dot(a, b, preferred_element_type=F32)


def norm(x, gain):
    mean = jnp.mean(x, axis=-1, keepdims=True)
    centred = x - mean
    var = jnp.mean(centred * centred, axis=-1, keepdims=True)
    return centred * lax.rsqrt(var + 1e-05) * gain


def head_rows():
    lane = lax.broadcasted_iota(jnp.int32, (HEADS, D), 1) // HEAD
    head = lax.broadcasted_iota(jnp.int32, (HEADS, D), 0)
    return jnp.where(lane == head, 1.0, 0.0).astype(F32)


def embed_kernel(ids_hbm, patches_hbm, weight_hbm, level_hbm, out_hbm, patches, weight, level, emb,
                 packed, ids, sems):
    copy_ids = pltpu.make_async_copy(ids_hbm, ids, sems.at[SH + 2 + LEVELS])
    copy_ids.start()
    copy_w = pltpu.make_async_copy(weight_hbm, weight, sems.at[SH])
    copy_w.start()
    rows = SW * LEVELS
    copies = []
    for b in range(SH):
        part = pl.ds(b * rows, rows)
        copy = pltpu.make_async_copy(patches_hbm.at[part], patches.at[part], sems.at[b])
        copy.start()
        copies.append(copy)
    copy_level = pltpu.make_async_copy(level_hbm, level, sems.at[SH + 1])
    copy_level.start()
    copy_w.wait()
    for b in range(SH):
        copies[b].wait()
        part = pl.ds(b * rows, rows)
        block = mm(patches[part, :], weight[...])
        for g in range(D // 128):
            emb[g, part, :] = block[:, g * 128 : (g + 1) * 128]
    copy_level.wait()
    copy_ids.wait()
    shift = level[...]
    sub = lax.broadcasted_iota(jnp.int32, (8, 128), 0)
    sends = []
    for m in range(LEVELS):
        tail = jnp.full(sub.shape, -1.0, F32)
        parts = []
        for s in range(CAP):
            slot = ids[s, 0, m]
            start = jnp.maximum(slot, 0) * rows + m
            picked = [emb[g, pl.ds(start, SW, stride=LEVELS), :] for g in range(D // 128)]
            parts.append(jnp.concatenate(picked, axis=1) + shift)
            tail = jnp.where(sub == s, slot.astype(F32), tail)
        rows_m = jnp.concatenate(parts, axis=0)
        groups = [rows_m[:, g * 128 : (g + 1) * 128] for g in range(GROUPS)]
        order = [v[:MAIN] for v in groups] + [v[MAIN:] for v in groups] + [tail]
        packed[m] = jnp.concatenate(order, axis=0).astype(BF16)
        send = pltpu.make_async_copy(packed.at[m], out_hbm.at[m], sems.at[SH + 2 + m])
        send.start()
        sends.append(send)
    for send in sends:
        send.wait()


def prep_kernel(own, other, far_a, far_b, pick_rows, pick_cols, spans, odd, mid_bias, edge_bias):
    is_odd = odd[0] == 1
    high_first = jnp.where(is_odd, 1, 2)
    row_a = pick_rows[high_first]
    row_b = pick_rows[3 - high_first]

    def codes(labels, row_pick, which, span):
        spread = mm(labels, row_pick) * pick_cols[which]
        return jnp.sum(spread, axis=0, keepdims=True) + spans[span : span + 1, :]

    def column(row):
        return jnp.broadcast_to(row, (8, 128)).T[:UNIT, :1]

    def bias(query, keys):
        return jnp.concatenate(
            [jnp.where(column(query) == k[:, :UNIT], 0.0, NEG) for k in keys], axis=1
        )

    for g in range(2):
        mine = codes(own[...], pick_rows[0], 0, g)
        theirs = codes(other[...], pick_rows[0], 0, g)
        mid_bias[g] = bias(mine, [mine, theirs])
    for e, (near, away, far) in enumerate(((row_a, row_b, far_a), (row_b, row_a, far_b))):
        mine = codes(own[...], near, 1, 2)
        theirs = codes(other[...], near, 1, 2)
        halo = codes(far[0], away, 1, 2)
        halo_other = codes(far[1], away, 1, 2)
        for g, (low, high) in enumerate(HALVES):
            parts = [k[:, low:high] for k in (mine, theirs, halo, halo_other)]
            keys = jnp.concatenate(parts, axis=1)
            edge_bias[e, g] = jnp.where(column(mine)[low:high] == keys, 0.0, NEG)


def cross_kernel(recv, gain, wq, w_kv, lq, w_out, swin_gain, to_unit, normed, edges,
                 edge_a, edge_b, mixed_hbm, mixed, sem):
    queries = (mm(lq[...], wq[...]) * ROOT).astype(BF16).astype(F32)
    mask = head_rows()
    masked = jnp.concatenate([queries[q : q + 1, :] * mask for q in range(LATENT)], axis=0)
    wkq = nt(w_kv[:, :D], masked.astype(BF16)).astype(BF16)
    main, rest, lists = [], [], []
    for l in range(LEVELS):
        tile = recv[l].astype(F32)
        main.append(
            jnp.concatenate([tile[g * MAIN : (g + 1) * MAIN] for g in range(GROUPS)], axis=1)
        )
        tail = tile[GROUPS * MAIN : GROUPS * SLOT_ROWS]
        rest.append(
            jnp.concatenate([tail[g * REST : (g + 1) * REST] for g in range(GROUPS)], axis=1)
        )
        lists.append(tile[GROUPS * SLOT_ROWS :])
    x = jnp.concatenate(main + rest, axis=0)
    keys_in = norm(x, gain[...]).astype(BF16)
    values = mm(keys_in, w_kv[:, D:]).astype(BF16).astype(F32)
    scores = mm(keys_in, wkq)
    row = lax.broadcasted_iota(jnp.int32, (MAIN, 128), 0)
    slot = jnp.where(row >= 2 * SW, 2, jnp.where(row >= SW, 1, 0))
    place = (row - slot * SW).astype(F32)
    tail_row = lax.broadcasted_iota(jnp.int32, (2 * REST, 128), 0)
    tail_place = (jnp.where(tail_row < REST, tail_row, tail_row - REST) + (SW - REST)).astype(F32)
    tags = []
    for ids in lists:
        block = jnp.where(slot == 0, ids[0:1], jnp.where(slot == 1, ids[1:2], ids[2:3]))
        tags.append(jnp.where(block >= 0, block * SW + place, -1.0))
    for l in range(0, LEVELS, 2):
        block = jnp.where(tail_row < REST, lists[l][2:3], lists[l + 1][2:3])
        tags.append(jnp.where(block >= 0, block * SW + tail_place, -1.0))
    tag = jnp.concatenate(tags, axis=0)
    lane = lax.broadcasted_iota(jnp.int32, (RECV, 128), 1).astype(F32)
    hit = jnp.where(tag == lane, 1.0, 0.0)
    hit_t = hit.T[:CELLS].astype(BF16)
    hit = hit.astype(BF16)
    present = tag[:, :64] >= 0
    weight = jnp.where(present, jnp.exp(scores), 0.0)

    def halves(v):
        high = v.astype(BF16)
        return jnp.concatenate([high.astype(F32), v - high.astype(F32)], axis=1).astype(BF16)

    total = mm(hit_t, halves(weight))
    total = total[:, :64] + total[:, 64:]
    spread = mm(hit[:, :CELLS], halves(total))
    spread = spread[:, :64] + spread[:, 64:]
    weight = (weight / jnp.where(present, spread, 1.0)).astype(BF16)
    starts = []
    for q in range(LATENT):
        pad = [jnp.zeros((HEADS, D), F32)] * LATENT
        pad[q] = mask
        wide = mm(weight, jnp.concatenate(pad, axis=0).astype(BF16))
        starts.append(mm(hit_t, (wide * values).astype(BF16)))
    mix = jnp.concatenate(starts, axis=0).astype(BF16)
    mixed[...] = mix
    keep = pltpu.make_async_copy(mixed, mixed_hbm, sem)
    keep.start()
    projected = mm(mix, w_out[...])
    queries = lq[...].astype(F32)
    start = jnp.concatenate(
        [projected[q * CELLS : (q + 1) * CELLS] + queries[q : q + 1] for q in range(LATENT)], axis=0
    )
    unit = norm(start, swin_gain[...]).astype(BF16)
    placed = mm(to_unit[...], unit)
    normed[...] = placed.astype(BF16)
    for e, edge in enumerate((edge_a, edge_b)):
        tokens = placed[(2 + e) * UNIT : (3 + e) * UNIT].astype(BF16)
        edges[e] = tokens
        edge[...] = tokens
    keep.wait()


def own_kernel(normed, mixed, w_qkv, w_out, lq, to_last, qkv, start, centre):
    centre[...] = normed[: 2 * UNIT, :]
    proj = mm(normed[...], w_qkv[...])
    qkv[:, :D] = proj[:, :D] * ROOT
    qkv[:, D:] = proj[:, D:]
    last = mm(to_last[...], mixed[...]).astype(BF16)
    level = lax.broadcasted_iota(jnp.int32, (TOKENS, D), 0) % LATENT
    queries = lq[...].astype(F32)
    rows = jnp.broadcast_to(queries[LATENT - 1 :], (TOKENS, D))
    for p in range(LATENT - 1):
        rows = jnp.where(level == p, queries[p : p + 1], rows)
    start[...] = mm(last, w_out[...]) + rows


def attend(queries, keys, values, bias):
    rows = queries.shape[0]
    lane = lax.broadcasted_iota(jnp.int32, (rows, 128), 1) // HEAD
    masks = [jnp.where(lane == h, 1.0, 0.0) for h in range(4)]
    outs = []
    tall = jnp.concatenate([bias] * 4, axis=0)
    queries = queries.astype(BF16).astype(F32)
    for g in range(4):
        cols = slice(g * 128, (g + 1) * 128)
        stack = jnp.concatenate([queries[:, cols] * m for m in masks], axis=0).astype(BF16)
        scores = nt(stack, keys[:, cols]) + tall
        top = jnp.max(scores, axis=-1, keepdims=True)
        exps = jnp.exp(scores - top)
        total = jnp.sum(exps, axis=-1, keepdims=True)
        part = mm(exps.astype(BF16), values[:, cols]) / total
        out = part[:rows] * masks[0]
        for h in range(1, 4):
            out = out + part[h * rows : (h + 1) * rows] * masks[h]
        outs.append(out)
    return jnp.concatenate(outs, axis=1)


def split_kernel(both, edge_a, edge_b):
    edge_a[...] = both[0]
    edge_b[...] = both[1]


def mid_kernel(other, other_edges, w_qkv, qkv, bias, other_kv, mix):
    tokens = [other[...].astype(F32), other_edges[0].astype(F32), other_edges[1].astype(F32)]
    theirs = mm(jnp.concatenate(tokens, axis=0).astype(BF16), w_qkv[:, D:])
    other_kv[...] = theirs[2 * UNIT :]
    for g in range(2):
        part = slice(g * UNIT, (g + 1) * UNIT)
        keys = jnp.concatenate([qkv[part, D : 2 * D], theirs[part, :D]], axis=0).astype(BF16)
        values = jnp.concatenate([qkv[part, 2 * D :], theirs[part, D:]], axis=0).astype(BF16)
        mix[part, :] = attend(qkv[part, :D], keys, values, bias[g])


def erf_gelu(v):
    return v * (1.0 + lax.erf(v * math.sqrt(0.5))) * 0.5


def last_kernel(near_a, far_a, near_b, far_b, w_qkv, qkv, other_kv, bias, mid, w_out, start, to_final, mlp_gain,
                w_up, w_down, out):
    parts = [mid[...]]
    upper = lax.broadcasted_iota(jnp.int32, (2 * HALF - UNIT, D), 0) < UNIT // 2 - HALVES[1][0]
    halos = [halo[...].astype(F32) for halo in (near_a, far_a, near_b, far_b)]
    halo_kv = mm(jnp.concatenate(halos, axis=0).astype(BF16), w_qkv[:, D:])
    for e in range(2):
        own = slice((2 + e) * UNIT, (3 + e) * UNIT)
        theirs = slice(e * UNIT, (e + 1) * UNIT)
        pieces = [qkv[own, D:], other_kv[theirs, :]]
        pieces += [halo_kv[(2 * e + i) * UNIT : (2 * e + i + 1) * UNIT] for i in range(2)]
        queries = qkv[own, :D]
        done = []
        for g, (low, high) in enumerate(HALVES):
            keys = jnp.concatenate([p[low:high, :D] for p in pieces], axis=0).astype(BF16)
            values = jnp.concatenate([p[low:high, D:] for p in pieces], axis=0).astype(BF16)
            done.append(attend(queries[low:high], keys, values, bias[e, g]))
        cut = HALVES[1][0]
        shared = jnp.where(upper, done[0][cut:], done[1][: HALF - cut])
        parts += [done[0][:cut], shared, done[1][HALF - cut :]]
    mix = jnp.concatenate(parts, axis=0).astype(BF16)
    mix = mm(to_final[...], mix).astype(BF16)
    attended = start[...] + mm(mix, w_out[...])
    mlp_in = norm(attended, mlp_gain[...]).astype(BF16)
    total = attended
    width = w_up.shape[1]
    step = 512
    for c in range(0, width, step):
        hidden = erf_gelu(mm(mlp_in, w_up[:, c : c + step])).astype(BF16)
        total = total + mm(hidden, w_down[c : c + step, :])
    for b in range(SH):
        for j in range(SW):
            at = (b * SW + j) * LATENT
            out[b, j] = total[at : at + LATENT]


def call(kernel, outs, *args, smem=(), hbm=(), hbm_out=(), scratch=(), limit=24, flops=10**9):
    specs = []
    for i in range(len(args)):
        space = pltpu.SMEM if i in smem else pltpu.HBM if i in hbm else pltpu.VMEM
        specs.append(pl.BlockSpec(memory_space=space))
    out_specs = [
        pl.BlockSpec(memory_space=pltpu.HBM if i in hbm_out else pltpu.VMEM) for i in range(len(outs))
    ]
    moved = sum(a.size * a.dtype.itemsize for a in args)
    return pl.pallas_call(
        kernel,
        out_shape=[jax.ShapeDtypeStruct(s, d) for s, d in outs],
        in_specs=specs,
        out_specs=out_specs,
        scratch_shapes=list(scratch),
        compiler_params=pltpu.CompilerParams(vmem_limit_bytes=limit << 20),
        cost_estimate=pl.CostEstimate(flops=flops, bytes_accessed=moved, transcendentals=0),
    )(*args)


def swap_pairs(change, turn=0):
    pairs = []
    for l in range(LEVELS):
        for a in range(4):
            for o in range(4):
                target = change(a, o)
                if target is not None:
                    level = l ^ turn if target == (a, o) else l
                    pairs.append(((l * 4 + a) * 4 + o, (level * 4 + target[0]) * 4 + target[1]))
    return pairs


def swap(block, pairs):
    return lax.ppermute(block, MESH_AXES, pairs)


def shards(patches, level_embed, embed_weight, block_ids, latent_queries, cross_gain, cross_query,
           cross_kv, cross_out, region_ids, swin_gain, swin_qkv, swin_out, mlp_gain, mlp_up, mlp_down):
    across = swap_pairs(lambda a, o: (a ^ 1, o))
    first = swap_pairs(lambda a, o: (a, o ^ 1))
    second = swap_pairs(lambda a, o: (a, 3 - o) if o in (1, 2) else None)
    second_all = swap_pairs(lambda a, o: (a, 3 - o) if o in (1, 2) else (a, o), turn=1)
    odd = lax.axis_index("lon") % 2
    features = patches.shape[-1]

    flat = patches[0].transpose(1, 2, 0, 3).reshape(SH * SW * LEVELS, features)
    ids = block_ids.transpose(0, 2, 4, 3, 1).reshape(CAP, 1, LEVELS)
    (packed,) = call(
        embed_kernel, [((LEVELS, SENT, 128), BF16)], ids, flat, embed_weight, level_embed,
        hbm=(0, 1, 2, 3), hbm_out=(0,), limit=63,
        scratch=[
            pltpu.VMEM((SH * SW * LEVELS, features), BF16),
            pltpu.VMEM((features, D), BF16),
            pltpu.VMEM((1, D), F32),
            pltpu.VMEM((D // 128, SH * SW * LEVELS, 128), F32),
            pltpu.VMEM((LEVELS, SENT, 128), BF16),
            pltpu.SMEM((CAP, 1, LEVELS), jnp.int32),
            pltpu.SemaphoreType.DMA((SH + 3 + LEVELS,)),
        ],
    )
    packed, region_ids, odd = lax.optimization_barrier((packed, region_ids, odd))
    received = lax.all_to_all(packed, "lvl", 0, 0, tiled=True)

    labels = jnp.pad(region_ids.astype(F32) + 1.0, ((0, 2), (0, 116)))
    other_labels = swap(labels, across)
    both = jnp.stack([labels, other_labels])
    far_labels_a, far_labels_b = swap(both, first), swap(both, second)
    rows, cols, spans = label_pickers()
    odd_one = odd.astype(jnp.int32).reshape(1)
    mid_bias, edge_bias = call(
        prep_kernel, [((2, UNIT, 2 * UNIT), F32), ((2, 2, HALF, 4 * HALF), F32)],
        labels, other_labels, far_labels_a, far_labels_b, rows, cols, spans, odd_one, smem=(7,),
    )
    to_unit_even, to_final_even = permutations(SW - EDGE)
    to_unit_odd, to_final_odd = permutations(0)
    to_unit = jnp.where(odd == 1, to_unit_odd, to_unit_even).astype(BF16)
    to_final = jnp.where(odd == 1, to_final_odd, to_final_even).astype(BF16)
    to_last = jnp.asarray(final_permutation(), BF16)

    received, mid_bias, edge_bias = lax.optimization_barrier((received, mid_bias, edge_bias))
    normed, edges, edge_a, edge_b, mixed = call(
        cross_kernel,
        [((TOKENS, D), BF16), ((2, UNIT, D), BF16)] + [((UNIT, D), BF16)] * 2 + [((TOKENS, D), BF16)],
        received, cross_gain[None], cross_query, cross_kv, latent_queries, cross_out, swin_gain[None],
        to_unit, hbm_out=(4,), flops=4 * 10**9,
        scratch=[pltpu.VMEM((TOKENS, D), BF16), pltpu.SemaphoreType.DMA],
    )
    other_edges = swap(edges, across)
    near_a, near_b = swap(edge_a, first), swap(edge_b, second_all)
    qkv, start, centre = call(
        own_kernel, [((TOKENS, 3 * D), F32), ((TOKENS, D), F32), ((2 * UNIT, D), BF16)],
        normed, mixed, swin_qkv, cross_out, latent_queries, to_last, flops=3 * 10**9,
    )
    other_centre = swap(centre, across)
    other_a, other_b = call(split_kernel, [((UNIT, D), BF16)] * 2, other_edges)
    far_a, far_b = swap(other_a, first), swap(other_b, second_all)
    other_kv, mid = call(
        mid_kernel, [((2 * UNIT, 2 * D), F32), ((2 * UNIT, D), F32)], other_centre, other_edges, swin_qkv, qkv, mid_bias,
        flops=3 * 10**9,
    )
    (out,) = call(
        last_kernel, [((SH, SW, LATENT, D), F32)],
        near_a, far_a, near_b, far_b, swin_qkv, qkv, other_kv, edge_bias, mid, swin_out, start, to_final,
        mlp_gain[None], mlp_up, mlp_down, flops=8 * 10**9,
    )
    return out.transpose(2, 0, 1, 3)


def solution(mesh):
    return jax.shard_map(
        shards,
        mesh=mesh,
        in_specs=(
            P("lvl", None, "lat", "lon", None), P("lvl", None), P(), P("lvl", None, "lat", "lon", None),
            P(), P(), P(), P(), P(), P(("lvl", "lat"), "lon"), P(), P(), P(), P(), P(), P(),
        ),
        out_specs=P(None, ("lvl", "lat"), "lon", None),
        check_vma=False,
    )
```

```python
import functools
import math

import jax
import jax.numpy as jnp
import numpy as np
from jax import lax
from jax.experimental import pallas as pl
from jax.experimental.pallas import tpu as pltpu
from jax.sharding import PartitionSpec as P

D = 512
HEADS = 16
HEAD = D // HEADS
ROOT = 1.0 / math.sqrt(HEAD)
LEVELS = 16
LATENT = 4
CAP = 3
SH = 6
SW = 12
EDGE = 3
CELLS = SH * SW
UNIT = 72
HALF = 40
HALVES = ((0, HALF), (UNIT - HALF, UNIT))
TOKENS = LATENT * CELLS
SLOT_ROWS = CAP * SW
MAIN = 32
REST = SLOT_ROWS - MAIN
GROUPS = D // 128
SENT = GROUPS * SLOT_ROWS + 8
RECV = LEVELS * SLOT_ROWS
MESH_AXES = ("lvl", "lat", "lon")
NEG = -1e30
F32 = jnp.float32
BF16 = jnp.bfloat16


def unit_tokens(first_edge):
    order = []
    for levels in ((0, 3), (1, 2)):
        order += [(p, b, EDGE + j) for p in levels for b in range(SH) for j in range(2 * EDGE)]
    for start in (first_edge, SW - EDGE - first_edge):
        order += [(p, b, start + j) for p in (0, 3, 1, 2) for b in range(SH) for j in range(EDGE)]
    return order


def permutations(first_edge):
    to_unit = np.zeros((TOKENS, TOKENS), np.float32)
    to_final = np.zeros((TOKENS, TOKENS), np.float32)
    for t, (p, b, j) in enumerate(unit_tokens(first_edge)):
        cell = b * SW + j
        to_unit[t, p * CELLS + cell] = 1
        to_final[cell * LATENT + p, t] = 1
    return to_unit, to_final


def final_permutation():
    out = np.zeros((TOKENS, TOKENS), np.float32)
    for cell in range(CELLS):
        for p in range(LATENT):
            out[cell * LATENT + p, p * CELLS + cell] = 1
    return out


def label_pickers():
    rows = np.zeros((3, 128, 128), np.float32)
    cols = np.zeros((2, 8, 128), np.float32)
    spans = np.zeros((8, 128), np.float32)
    tokens = unit_tokens(0)
    window = [(p + 1) // 2 for p in range(LATENT)]
    for i in range(UNIT):
        _, b, j = tokens[i]
        rows[0, j, i] = 1
        cols[0, b, i] = 1
        for u in range(3):
            spans[u, i] = 4 * window[tokens[u * UNIT + i][0]]
        _, b, j = tokens[2 * UNIT + i]
        rows[1, j, i] = 1
        rows[2, j + SW - EDGE, i] = 1
        cols[1, b, i] = 1
    return rows, cols, spans


def nt(a, b):
    return lax.dot_general(a, b, (((1,), (1,)), ((), ())), preferred_element_type=F32)


def mm(a, b):
    return jnp.dot(a, b, preferred_element_type=F32)


def norm(x, gain):
    mean = jnp.mean(x, axis=-1, keepdims=True)
    centred = x - mean
    var = jnp.mean(centred * centred, axis=-1, keepdims=True)
    return centred * lax.rsqrt(var + 1e-05) * gain


def head_rows():
    lane = lax.broadcasted_iota(jnp.int32, (HEADS, D), 1) // HEAD
    head = lax.broadcasted_iota(jnp.int32, (HEADS, D), 0)
    return jnp.where(lane == head, 1.0, 0.0).astype(F32)


def embed_kernel(ids_hbm, patches_hbm, weight_hbm, level_hbm, out_hbm, patches, weight, level, emb,
                 packed, ids, sems):
    copy_ids = pltpu.make_async_copy(ids_hbm, ids, sems.at[SH + 2 + LEVELS])
    copy_ids.start()
    copy_w = pltpu.make_async_copy(weight_hbm, weight, sems.at[SH])
    copy_w.start()
    rows = SW * LEVELS
    copies = []
    for b in range(SH):
        part = pl.ds(b * rows, rows)
        copy = pltpu.make_async_copy(patches_hbm.at[part], patches.at[part], sems.at[b])
        copy.start()
        copies.append(copy)
    copy_level = pltpu.make_async_copy(level_hbm, level, sems.at[SH + 1])
    copy_level.start()
    copy_w.wait()
    for b in range(SH):
        copies[b].wait()
        part = pl.ds(b * rows, rows)
        block = mm(patches[part, :], weight[...])
        for g in range(D // 128):
            emb[g, part, :] = block[:, g * 128 : (g + 1) * 128]
    copy_level.wait()
    copy_ids.wait()
    shift = level[...]
    sub = lax.broadcasted_iota(jnp.int32, (8, 128), 0)
    sends = []
    for m in range(LEVELS):
        tail = jnp.full(sub.shape, -1.0, F32)
        parts = []
        for s in range(CAP):
            slot = ids[s, 0, m]
            start = jnp.maximum(slot, 0) * rows + m
            picked = [emb[g, pl.ds(start, SW, stride=LEVELS), :] for g in range(D // 128)]
            parts.append(jnp.concatenate(picked, axis=1) + shift)
            tail = jnp.where(sub == s, slot.astype(F32), tail)
        rows_m = jnp.concatenate(parts, axis=0)
        groups = [rows_m[:, g * 128 : (g + 1) * 128] for g in range(GROUPS)]
        order = [v[:MAIN] for v in groups] + [v[MAIN:] for v in groups] + [tail]
        packed[m] = jnp.concatenate(order, axis=0).astype(BF16)
        send = pltpu.make_async_copy(packed.at[m], out_hbm.at[m], sems.at[SH + 2 + m])
        send.start()
        sends.append(send)
    for send in sends:
        send.wait()


def prep_kernel(own, other, far_a, far_b, pick_rows, pick_cols, spans, odd, mid_bias, edge_bias):
    is_odd = odd[0] == 1
    high_first = jnp.where(is_odd, 1, 2)
    row_a = pick_rows[high_first]
    row_b = pick_rows[3 - high_first]

    def codes(labels, row_pick, which, span):
        spread = mm(labels, row_pick) * pick_cols[which]
        return jnp.sum(spread, axis=0, keepdims=True) + spans[span : span + 1, :]

    def column(row):
        return jnp.broadcast_to(row, (8, 128)).T[:UNIT, :1]

    def bias(query, keys):
        return jnp.concatenate(
            [jnp.where(column(query) == k[:, :UNIT], 0.0, NEG) for k in keys], axis=1
        )

    for g in range(2):
        mine = codes(own[...], pick_rows[0], 0, g)
        theirs = codes(other[...], pick_rows[0], 0, g)
        mid_bias[g] = bias(mine, [mine, theirs])
    for e, (near, away, far) in enumerate(((row_a, row_b, far_a), (row_b, row_a, far_b))):
        mine = codes(own[...], near, 1, 2)
        theirs = codes(other[...], near, 1, 2)
        halo = codes(far[0], away, 1, 2)
        halo_other = codes(far[1], away, 1, 2)
        for g, (low, high) in enumerate(HALVES):
            parts = [k[:, low:high] for k in (mine, theirs, halo, halo_other)]
            keys = jnp.concatenate(parts, axis=1)
            edge_bias[e, g] = jnp.where(column(mine)[low:high] == keys, 0.0, NEG)


def cross_kernel(recv, gain, wq, w_kv, lq, w_out, swin_gain, to_unit, normed, edges,
                 edge_a, edge_b, mixed_hbm, mixed, sem):
    queries = (mm(lq[...], wq[...]) * ROOT).astype(BF16).astype(F32)
    mask = head_rows()
    masked = jnp.concatenate([queries[q : q + 1, :] * mask for q in range(LATENT)], axis=0)
    wkq = nt(w_kv[:, :D], masked.astype(BF16)).astype(BF16)
    main, rest, lists = [], [], []
    for l in range(LEVELS):
        tile = recv[l].astype(F32)
        main.append(
            jnp.concatenate([tile[g * MAIN : (g + 1) * MAIN] for g in range(GROUPS)], axis=1)
        )
        tail = tile[GROUPS * MAIN : GROUPS * SLOT_ROWS]
        rest.append(
            jnp.concatenate([tail[g * REST : (g + 1) * REST] for g in range(GROUPS)], axis=1)
        )
        lists.append(tile[GROUPS * SLOT_ROWS :])
    x = jnp.concatenate(main + rest, axis=0)
    keys_in = norm(x, gain[...]).astype(BF16)
    values = mm(keys_in, w_kv[:, D:]).astype(BF16).astype(F32)
    scores = mm(keys_in, wkq)
    row = lax.broadcasted_iota(jnp.int32, (MAIN, 128), 0)
    slot = jnp.where(row >= 2 * SW, 2, jnp.where(row >= SW, 1, 0))
    place = (row - slot * SW).astype(F32)
    tail_row = lax.broadcasted_iota(jnp.int32, (2 * REST, 128), 0)
    tail_place = (jnp.where(tail_row < REST, tail_row, tail_row - REST) + (SW - REST)).astype(F32)
    tags = []
    for ids in lists:
        block = jnp.where(slot == 0, ids[0:1], jnp.where(slot == 1, ids[1:2], ids[2:3]))
        tags.append(jnp.where(block >= 0, block * SW + place, -1.0))
    for l in range(0, LEVELS, 2):
        block = jnp.where(tail_row < REST, lists[l][2:3], lists[l + 1][2:3])
        tags.append(jnp.where(block >= 0, block * SW + tail_place, -1.0))
    tag = jnp.concatenate(tags, axis=0)
    lane = lax.broadcasted_iota(jnp.int32, (RECV, 128), 1).astype(F32)
    hit = jnp.where(tag == lane, 1.0, 0.0)
    hit_t = hit.T[:CELLS].astype(BF16)
    hit = hit.astype(BF16)
    present = tag[:, :64] >= 0
    weight = jnp.where(present, jnp.exp(scores), 0.0)

    def halves(v):
        high = v.astype(BF16)
        return jnp.concatenate([high.astype(F32), v - high.astype(F32)], axis=1).astype(BF16)

    total = mm(hit_t, halves(weight))
    total = total[:, :64] + total[:, 64:]
    spread = mm(hit[:, :CELLS], halves(total))
    spread = spread[:, :64] + spread[:, 64:]
    weight = (weight / jnp.where(present, spread, 1.0)).astype(BF16)
    starts = []
    for q in range(LATENT):
        pad = [jnp.zeros((HEADS, D), F32)] * LATENT
        pad[q] = mask
        wide = mm(weight, jnp.concatenate(pad, axis=0).astype(BF16)).astype(BF16)
        starts.append(mm(hit_t, wide * values.astype(BF16)))
    mix = jnp.concatenate(starts, axis=0).astype(BF16)
    mixed[...] = mix
    keep = pltpu.make_async_copy(mixed, mixed_hbm, sem)
    keep.start()
    projected = mm(mix, w_out[...])
    queries = lq[...].astype(F32)
    start = jnp.concatenate(
        [projected[q * CELLS : (q + 1) * CELLS] + queries[q : q + 1] for q in range(LATENT)], axis=0
    )
    unit = norm(start, swin_gain[...]).astype(BF16)
    placed = mm(to_unit[...], unit)
    normed[...] = placed.astype(BF16)
    for e, edge in enumerate((edge_a, edge_b)):
        tokens = placed[(2 + e) * UNIT : (3 + e) * UNIT].astype(BF16)
        edges[e] = tokens
        edge[...] = tokens
    keep.wait()


def own_kernel(normed, mixed, w_qkv, w_out, lq, to_last, w_up, w_down, qkv, start, centre):
    centre[...] = normed[: 2 * UNIT, :]
    proj = mm(normed[...], w_qkv[...])
    qkv[:, :D] = proj[:, :D] * ROOT
    qkv[:, D:] = proj[:, D:]
    last = mm(to_last[...], mixed[...]).astype(BF16)
    level = lax.broadcasted_iota(jnp.int32, (TOKENS, D), 0) % LATENT
    queries = lq[...].astype(F32)
    rows = jnp.broadcast_to(queries[LATENT - 1 :], (TOKENS, D))
    for p in range(LATENT - 1):
        rows = jnp.where(level == p, queries[p : p + 1], rows)
    start[...] = mm(last, w_out[...]) + rows


def attend(queries, keys, values, bias):
    rows = queries.shape[0]
    lane = lax.broadcasted_iota(jnp.int32, (rows, 128), 1) // HEAD
    masks = [jnp.where(lane == h, 1.0, 0.0) for h in range(4)]
    outs = []
    tall = jnp.concatenate([bias] * 4, axis=0)
    queries = queries.astype(BF16).astype(F32)
    for g in range(4):
        cols = slice(g * 128, (g + 1) * 128)
        stack = jnp.concatenate([queries[:, cols] * m for m in masks], axis=0).astype(BF16)
        scores = nt(stack, keys[:, cols]) + tall
        top = jnp.max(scores, axis=-1, keepdims=True)
        exps = jnp.exp(scores - top)
        total = jnp.sum(exps, axis=-1, keepdims=True)
        part = mm(exps.astype(BF16), values[:, cols]) / total
        out = part[:rows] * masks[0]
        for h in range(1, 4):
            out = out + part[h * rows : (h + 1) * rows] * masks[h]
        outs.append(out)
    return jnp.concatenate(outs, axis=1)


def split_kernel(both, edge_a, edge_b):
    edge_a[...] = both[0]
    edge_b[...] = both[1]


def mid_kernel(other, other_edges, w_qkv, qkv, bias, other_kv, mix):
    tokens = [other[...].astype(F32), other_edges[0].astype(F32), other_edges[1].astype(F32)]
    theirs = mm(jnp.concatenate(tokens, axis=0).astype(BF16), w_qkv[:, D:])
    other_kv[...] = theirs[2 * UNIT :]
    for g in range(2):
        part = slice(g * UNIT, (g + 1) * UNIT)
        keys = jnp.concatenate([qkv[part, D : 2 * D], theirs[part, :D]], axis=0).astype(BF16)
        values = jnp.concatenate([qkv[part, 2 * D :], theirs[part, D:]], axis=0).astype(BF16)
        mix[part, :] = attend(qkv[part, :D], keys, values, bias[g])


def erf_gelu(v):
    return v * (1.0 + lax.erf(v * math.sqrt(0.5))) * 0.5


def last_kernel(near_a, far_a, near_b, far_b, w_qkv, qkv, other_kv, bias, mid, w_out, start, to_final, mlp_gain,
                w_up, w_down, out):
    parts = [mid[...]]
    upper = lax.broadcasted_iota(jnp.int32, (2 * HALF - UNIT, D), 0) < UNIT // 2 - HALVES[1][0]
    halos = [halo[...].astype(F32) for halo in (near_a, far_a, near_b, far_b)]
    halo_kv = mm(jnp.concatenate(halos, axis=0).astype(BF16), w_qkv[:, D:])
    for e in range(2):
        own = slice((2 + e) * UNIT, (3 + e) * UNIT)
        theirs = slice(e * UNIT, (e + 1) * UNIT)
        pieces = [qkv[own, D:], other_kv[theirs, :]]
        pieces += [halo_kv[(2 * e + i) * UNIT : (2 * e + i + 1) * UNIT] for i in range(2)]
        queries = qkv[own, :D]
        done = []
        for g, (low, high) in enumerate(HALVES):
            keys = jnp.concatenate([p[low:high, :D] for p in pieces], axis=0).astype(BF16)
            values = jnp.concatenate([p[low:high, D:] for p in pieces], axis=0).astype(BF16)
            done.append(attend(queries[low:high], keys, values, bias[e, g]))
        cut = HALVES[1][0]
        shared = jnp.where(upper, done[0][cut:], done[1][: HALF - cut])
        parts += [done[0][:cut], shared, done[1][HALF - cut :]]
    mix = jnp.concatenate(parts, axis=0).astype(BF16)
    mix = mm(to_final[...], mix).astype(BF16)
    attended = start[...] + mm(mix, w_out[...])
    mlp_in = norm(attended, mlp_gain[...]).astype(BF16)
    total = attended
    width = w_up.shape[1]
    step = 2048
    for c in range(0, width, step):
        hidden = erf_gelu(mm(mlp_in, w_up[:, c : c + step])).astype(BF16)
        total = total + mm(hidden, w_down[c : c + step, :])
    for b in range(SH):
        for j in range(SW):
            at = (b * SW + j) * LATENT
            out[b, j] = total[at : at + LATENT]


def call(kernel, outs, *args, smem=(), hbm=(), hbm_out=(), scratch=(), limit=24, flops=10**9):
    specs = []
    for i in range(len(args)):
        space = pltpu.SMEM if i in smem else pltpu.HBM if i in hbm else pltpu.VMEM
        specs.append(pl.BlockSpec(memory_space=space))
    out_specs = [
        pl.BlockSpec(memory_space=pltpu.HBM if i in hbm_out else pltpu.VMEM) for i in range(len(outs))
    ]
    moved = sum(a.size * a.dtype.itemsize for a in args)
    return pl.pallas_call(
        kernel,
        out_shape=[jax.ShapeDtypeStruct(s, d) for s, d in outs],
        in_specs=specs,
        out_specs=out_specs,
        scratch_shapes=list(scratch),
        compiler_params=pltpu.CompilerParams(vmem_limit_bytes=limit << 20),
        cost_estimate=pl.CostEstimate(flops=flops, bytes_accessed=moved, transcendentals=0),
    )(*args)


def swap_pairs(change, turn=0):
    pairs = []
    for l in range(LEVELS):
        for a in range(4):
            for o in range(4):
                target = change(a, o)
                if target is not None:
                    level = l ^ turn if target == (a, o) else l
                    pairs.append(((l * 4 + a) * 4 + o, (level * 4 + target[0]) * 4 + target[1]))
    return pairs


def swap(block, pairs):
    return lax.ppermute(block, MESH_AXES, pairs)


def shards(patches, level_embed, embed_weight, block_ids, latent_queries, cross_gain, cross_query,
           cross_kv, cross_out, region_ids, swin_gain, swin_qkv, swin_out, mlp_gain, mlp_up, mlp_down):
    across = swap_pairs(lambda a, o: (a ^ 1, o))
    first = swap_pairs(lambda a, o: (a, o ^ 1))
    second = swap_pairs(lambda a, o: (a, 3 - o) if o in (1, 2) else None)
    second_all = swap_pairs(lambda a, o: (a, 3 - o) if o in (1, 2) else (a, o), turn=1)
    odd = lax.axis_index("lon") % 2
    features = patches.shape[-1]

    flat = patches[0].transpose(1, 2, 0, 3).reshape(SH * SW * LEVELS, features)
    ids = block_ids.transpose(0, 2, 4, 3, 1).reshape(CAP, 1, LEVELS)
    (packed,) = call(
        embed_kernel, [((LEVELS, SENT, 128), BF16)], ids, flat, embed_weight, level_embed,
        hbm=(0, 1, 2, 3), hbm_out=(0,), limit=63,
        scratch=[
            pltpu.VMEM((SH * SW * LEVELS, features), BF16),
            pltpu.VMEM((features, D), BF16),
            pltpu.VMEM((1, D), F32),
            pltpu.VMEM((D // 128, SH * SW * LEVELS, 128), F32),
            pltpu.VMEM((LEVELS, SENT, 128), BF16),
            pltpu.SMEM((CAP, 1, LEVELS), jnp.int32),
            pltpu.SemaphoreType.DMA((SH + 3 + LEVELS,)),
        ],
    )
    packed, region_ids, odd = lax.optimization_barrier((packed, region_ids, odd))
    received = lax.all_to_all(packed, "lvl", 0, 0, tiled=True)

    labels = jnp.pad(region_ids.astype(F32) + 1.0, ((0, 2), (0, 116)))
    other_labels = swap(labels, across)
    both = jnp.stack([labels, other_labels])
    far_labels_a, far_labels_b = swap(both, first), swap(both, second)
    rows, cols, spans = label_pickers()
    odd_one = odd.astype(jnp.int32).reshape(1)
    mid_bias, edge_bias = call(
        prep_kernel, [((2, UNIT, 2 * UNIT), F32), ((2, 2, HALF, 4 * HALF), F32)],
        labels, other_labels, far_labels_a, far_labels_b, rows, cols, spans, odd_one, smem=(7,),
    )
    to_unit_even, to_final_even = permutations(SW - EDGE)
    to_unit_odd, to_final_odd = permutations(0)
    to_unit = jnp.where(odd == 1, to_unit_odd, to_unit_even).astype(BF16)
    to_final = jnp.where(odd == 1, to_final_odd, to_final_even).astype(BF16)
    to_last = jnp.asarray(final_permutation(), BF16)

    received, mid_bias, edge_bias = lax.optimization_barrier((received, mid_bias, edge_bias))
    normed, edges, edge_a, edge_b, mixed = call(
        cross_kernel,
        [((TOKENS, D), BF16), ((2, UNIT, D), BF16)] + [((UNIT, D), BF16)] * 2 + [((TOKENS, D), BF16)],
        received, cross_gain[None], cross_query, cross_kv, latent_queries, cross_out, swin_gain[None],
        to_unit, hbm_out=(4,), flops=4 * 10**9,
        scratch=[pltpu.VMEM((TOKENS, D), BF16), pltpu.SemaphoreType.DMA],
    )
    other_edges = swap(edges, across)
    near_a, near_b = swap(edge_a, first), swap(edge_b, second_all)
    qkv, start, centre = call(
        own_kernel, [((TOKENS, 3 * D), F32), ((TOKENS, D), F32), ((2 * UNIT, D), BF16)],
        normed, mixed, swin_qkv, cross_out, latent_queries, to_last, mlp_up, mlp_down, flops=3 * 10**9,
    )
    other_centre = swap(centre, across)
    other_a, other_b = call(split_kernel, [((UNIT, D), BF16)] * 2, other_edges)
    far_a, far_b = swap(other_a, first), swap(other_b, second_all)
    other_kv, mid = call(
        mid_kernel, [((2 * UNIT, 2 * D), F32), ((2 * UNIT, D), F32)], other_centre, other_edges, swin_qkv, qkv, mid_bias,
        flops=3 * 10**9,
    )
    (out,) = call(
        last_kernel, [((SH, SW, LATENT, D), F32)],
        near_a, far_a, near_b, far_b, swin_qkv, qkv, other_kv, edge_bias, mid, swin_out, start, to_final,
        mlp_gain[None], mlp_up, mlp_down, flops=8 * 10**9,
    )
    return out.transpose(2, 0, 1, 3)


def solution(mesh):
    return jax.shard_map(
        shards,
        mesh=mesh,
        in_specs=(
            P("lvl", None, "lat", "lon", None), P("lvl", None), P(), P("lvl", None, "lat", "lon", None),
            P(), P(), P(), P(), P(), P(("lvl", "lat"), "lon"), P(), P(), P(), P(), P(), P(),
        ),
        out_specs=P(None, ("lvl", "lat"), "lon", None),
        check_vma=False,
    )
```

```python
import functools
import math

import jax
import jax.numpy as jnp
import numpy as np
from jax import lax
from jax.experimental import pallas as pl
from jax.experimental.pallas import tpu as pltpu
from jax.sharding import PartitionSpec as P

D = 512
HEADS = 16
HEAD = D // HEADS
ROOT = 1.0 / math.sqrt(HEAD)
LEVELS = 16
LATENT = 4
CAP = 3
SH = 6
SW = 12
EDGE = 3
CELLS = SH * SW
UNIT = 72
HALF = 40
HALVES = ((0, HALF), (UNIT - HALF, UNIT))
TOKENS = LATENT * CELLS
SLOT_ROWS = CAP * SW
MAIN = 32
REST = SLOT_ROWS - MAIN
GROUPS = D // 128
SENT = GROUPS * SLOT_ROWS + 8
RECV = LEVELS * SLOT_ROWS
MESH_AXES = ("lvl", "lat", "lon")
NEG = -1e30
F32 = jnp.float32
BF16 = jnp.bfloat16


def unit_tokens(first_edge):
    order = []
    for levels in ((0, 3), (1, 2)):
        order += [(p, b, EDGE + j) for p in levels for b in range(SH) for j in range(2 * EDGE)]
    for start in (first_edge, SW - EDGE - first_edge):
        order += [(p, b, start + j) for p in (0, 3, 1, 2) for b in range(SH) for j in range(EDGE)]
    return order


def permutations(first_edge):
    to_unit = np.zeros((TOKENS, TOKENS), np.float32)
    to_final = np.zeros((TOKENS, TOKENS), np.float32)
    for t, (p, b, j) in enumerate(unit_tokens(first_edge)):
        cell = b * SW + j
        to_unit[t, p * CELLS + cell] = 1
        to_final[cell * LATENT + p, t] = 1
    return to_unit, to_final


def final_permutation():
    out = np.zeros((TOKENS, TOKENS), np.float32)
    for cell in range(CELLS):
        for p in range(LATENT):
            out[cell * LATENT + p, p * CELLS + cell] = 1
    return out


def label_pickers():
    rows = np.zeros((3, 128, 128), np.float32)
    cols = np.zeros((2, 8, 128), np.float32)
    spans = np.zeros((8, 128), np.float32)
    tokens = unit_tokens(0)
    window = [(p + 1) // 2 for p in range(LATENT)]
    for i in range(UNIT):
        _, b, j = tokens[i]
        rows[0, j, i] = 1
        cols[0, b, i] = 1
        for u in range(3):
            spans[u, i] = 4 * window[tokens[u * UNIT + i][0]]
        _, b, j = tokens[2 * UNIT + i]
        rows[1, j, i] = 1
        rows[2, j + SW - EDGE, i] = 1
        cols[1, b, i] = 1
    return rows, cols, spans


def nt(a, b):
    return lax.dot_general(a, b, (((1,), (1,)), ((), ())), preferred_element_type=F32)


def mm(a, b):
    return jnp.dot(a, b, preferred_element_type=F32)


def norm(x, gain):
    mean = jnp.mean(x, axis=-1, keepdims=True)
    centred = x - mean
    var = jnp.mean(centred * centred, axis=-1, keepdims=True)
    return centred * lax.rsqrt(var + 1e-05) * gain


def head_rows():
    lane = lax.broadcasted_iota(jnp.int32, (HEADS, D), 1) // HEAD
    head = lax.broadcasted_iota(jnp.int32, (HEADS, D), 0)
    return jnp.where(lane == head, 1.0, 0.0).astype(F32)


def embed_kernel(ids_hbm, patches_hbm, weight_hbm, level_hbm, out_hbm, patches, weight, level, emb,
                 packed, ids, sems):
    copy_ids = pltpu.make_async_copy(ids_hbm, ids, sems.at[SH + 2 + LEVELS])
    copy_ids.start()
    copy_w = pltpu.make_async_copy(weight_hbm, weight, sems.at[SH])
    copy_w.start()
    rows = SW * LEVELS
    copies = []
    for b in range(SH):
        part = pl.ds(b * rows, rows)
        copy = pltpu.make_async_copy(patches_hbm.at[part], patches.at[part], sems.at[b])
        copy.start()
        copies.append(copy)
    copy_level = pltpu.make_async_copy(level_hbm, level, sems.at[SH + 1])
    copy_level.start()
    copy_w.wait()
    for b in range(0, SH, 3):
        for k in range(b, b + 3):
            copies[k].wait()
        part = pl.ds(b * rows, 3 * rows)
        block = mm(patches[part, :], weight[...])
        for g in range(D // 128):
            emb[g, part, :] = block[:, g * 128 : (g + 1) * 128]
    copy_level.wait()
    copy_ids.wait()
    shift = level[...]
    sub = lax.broadcasted_iota(jnp.int32, (8, 128), 0)
    sends = []
    for m in range(LEVELS):
        tail = jnp.full(sub.shape, -1.0, F32)
        parts = []
        for s in range(CAP):
            slot = ids[s, 0, m]
            start = jnp.maximum(slot, 0) * rows + m
            picked = [emb[g, pl.ds(start, SW, stride=LEVELS), :] for g in range(D // 128)]
            parts.append(jnp.concatenate(picked, axis=1) + shift)
            tail = jnp.where(sub == s, slot.astype(F32), tail)
        rows_m = jnp.concatenate(parts, axis=0)
        groups = [rows_m[:, g * 128 : (g + 1) * 128] for g in range(GROUPS)]
        order = [v[:MAIN] for v in groups] + [v[MAIN:] for v in groups] + [tail]
        packed[m] = jnp.concatenate(order, axis=0).astype(BF16)
        send = pltpu.make_async_copy(packed.at[m], out_hbm.at[m], sems.at[SH + 2 + m])
        send.start()
        sends.append(send)
    for send in sends:
        send.wait()


def prep_kernel(own, other, far_a, far_b, pick_rows, pick_cols, spans, odd, mid_bias, edge_bias):
    is_odd = odd[0] == 1
    high_first = jnp.where(is_odd, 1, 2)
    row_a = pick_rows[high_first]
    row_b = pick_rows[3 - high_first]

    def codes(labels, row_pick, which, span):
        spread = mm(labels, row_pick) * pick_cols[which]
        return jnp.sum(spread, axis=0, keepdims=True) + spans[span : span + 1, :]

    def column(row):
        return jnp.broadcast_to(row, (8, 128)).T[:UNIT, :1]

    def bias(query, keys):
        return jnp.concatenate(
            [jnp.where(column(query) == k[:, :UNIT], 0.0, NEG) for k in keys], axis=1
        )

    for g in range(2):
        mine = codes(own[...], pick_rows[0], 0, g)
        theirs = codes(other[...], pick_rows[0], 0, g)
        mid_bias[g] = bias(mine, [mine, theirs])
    for e, (near, away, far) in enumerate(((row_a, row_b, far_a), (row_b, row_a, far_b))):
        mine = codes(own[...], near, 1, 2)
        theirs = codes(other[...], near, 1, 2)
        halo = codes(far[0], away, 1, 2)
        halo_other = codes(far[1], away, 1, 2)
        for g, (low, high) in enumerate(HALVES):
            parts = [k[:, low:high] for k in (mine, theirs, halo, halo_other)]
            keys = jnp.concatenate(parts, axis=1)
            edge_bias[e, g] = jnp.where(column(mine)[low:high] == keys, 0.0, NEG)


def cross_kernel(recv, gain, wq, w_kv, lq, w_out, swin_gain, to_unit, normed, edges,
                 edge_a, edge_b, mixed_hbm, mixed, sem):
    queries = (mm(lq[...], wq[...]) * ROOT).astype(BF16).astype(F32)
    mask = head_rows()
    masked = jnp.concatenate([queries[q : q + 1, :] * mask for q in range(LATENT)], axis=0)
    wkq = nt(w_kv[:, :D], masked.astype(BF16)).astype(BF16)
    main, rest, lists = [], [], []
    for l in range(LEVELS):
        tile = recv[l].astype(F32)
        main.append(
            jnp.concatenate([tile[g * MAIN : (g + 1) * MAIN] for g in range(GROUPS)], axis=1)
        )
        tail = tile[GROUPS * MAIN : GROUPS * SLOT_ROWS]
        rest.append(
            jnp.concatenate([tail[g * REST : (g + 1) * REST] for g in range(GROUPS)], axis=1)
        )
        lists.append(tile[GROUPS * SLOT_ROWS :])
    x = jnp.concatenate(main + rest, axis=0)
    keys_in = norm(x, gain[...]).astype(BF16)
    values = mm(keys_in, w_kv[:, D:]).astype(BF16).astype(F32)
    scores = mm(keys_in, wkq)
    row = lax.broadcasted_iota(jnp.int32, (MAIN, 128), 0)
    slot = jnp.where(row >= 2 * SW, 2, jnp.where(row >= SW, 1, 0))
    place = (row - slot * SW).astype(F32)
    tail_row = lax.broadcasted_iota(jnp.int32, (2 * REST, 128), 0)
    tail_place = (jnp.where(tail_row < REST, tail_row, tail_row - REST) + (SW - REST)).astype(F32)
    tags = []
    for ids in lists:
        block = jnp.where(slot == 0, ids[0:1], jnp.where(slot == 1, ids[1:2], ids[2:3]))
        tags.append(jnp.where(block >= 0, block * SW + place, -1.0))
    for l in range(0, LEVELS, 2):
        block = jnp.where(tail_row < REST, lists[l][2:3], lists[l + 1][2:3])
        tags.append(jnp.where(block >= 0, block * SW + tail_place, -1.0))
    tag = jnp.concatenate(tags, axis=0)
    lane = lax.broadcasted_iota(jnp.int32, (RECV, 128), 1).astype(F32)
    hit = jnp.where(tag == lane, 1.0, 0.0)
    hit_t = hit.T[:CELLS].astype(BF16)
    hit = hit.astype(BF16)
    present = tag[:, :64] >= 0
    weight = jnp.where(present, jnp.exp(scores), 0.0)

    def halves(v):
        high = v.astype(BF16)
        return jnp.concatenate([high.astype(F32), v - high.astype(F32)], axis=1).astype(BF16)

    total = mm(hit_t, halves(weight))
    total = total[:, :64] + total[:, 64:]
    spread = mm(hit[:, :CELLS], halves(total))
    spread = spread[:, :64] + spread[:, 64:]
    weight = (weight / jnp.where(present, spread, 1.0)).astype(BF16)
    starts = []
    for q in range(LATENT):
        pad = [jnp.zeros((HEADS, D), F32)] * LATENT
        pad[q] = mask
        wide = mm(weight, jnp.concatenate(pad, axis=0).astype(BF16)).astype(BF16)
        starts.append(mm(hit_t, wide * values.astype(BF16)))
    mix = jnp.concatenate(starts, axis=0).astype(BF16)
    mixed[...] = mix
    keep = pltpu.make_async_copy(mixed, mixed_hbm, sem)
    keep.start()
    projected = mm(mix, w_out[...])
    queries = lq[...].astype(F32)
    start = jnp.concatenate(
        [projected[q * CELLS : (q + 1) * CELLS] + queries[q : q + 1] for q in range(LATENT)], axis=0
    )
    unit = norm(start, swin_gain[...]).astype(BF16)
    placed = mm(to_unit[...], unit)
    normed[...] = placed.astype(BF16)
    for e, edge in enumerate((edge_a, edge_b)):
        tokens = placed[(2 + e) * UNIT : (3 + e) * UNIT].astype(BF16)
        edges[e] = tokens
        edge[...] = tokens
    keep.wait()


def own_kernel(normed, mixed, w_qkv, w_out, lq, to_last, w_up, w_down, qkv, start, centre):
    centre[...] = normed[: 2 * UNIT, :]
    proj = mm(normed[...], w_qkv[...])
    qkv[:, :D] = proj[:, :D] * ROOT
    qkv[:, D:] = proj[:, D:]
    last = mm(to_last[...], mixed[...]).astype(BF16)
    level = lax.broadcasted_iota(jnp.int32, (TOKENS, D), 0) % LATENT
    queries = lq[...].astype(F32)
    rows = jnp.broadcast_to(queries[LATENT - 1 :], (TOKENS, D))
    for p in range(LATENT - 1):
        rows = jnp.where(level == p, queries[p : p + 1], rows)
    start[...] = mm(last, w_out[...]) + rows


def attend(queries, keys, values, bias):
    rows = queries.shape[0]
    lane = lax.broadcasted_iota(jnp.int32, (rows, 128), 1) // HEAD
    masks = [jnp.where(lane == h, 1.0, 0.0) for h in range(4)]
    outs = []
    tall = jnp.concatenate([bias] * 4, axis=0)
    for g in range(4):
        cols = slice(g * 128, (g + 1) * 128)
        stack = jnp.concatenate([jnp.where(lane == h, queries[:, cols], 0.0) for h in range(4)], axis=0).astype(BF16)
        scores = nt(stack, keys[:, cols]) + tall
        top = jnp.max(scores, axis=-1, keepdims=True)
        exps = jnp.exp(scores - top)
        total = jnp.sum(exps, axis=-1, keepdims=True)
        part = mm(exps.astype(BF16), values[:, cols])
        out, scale = part[:rows], jnp.broadcast_to(total[:rows], (rows, 128))
        for h in range(1, 4):
            here = slice(h * rows, (h + 1) * rows)
            out = jnp.where(lane == h, part[here], out)
            scale = jnp.where(lane == h, total[here], scale)
        outs.append(out / scale)
    return jnp.concatenate(outs, axis=1)


def split_kernel(both, edge_a, edge_b):
    edge_a[...] = both[0]
    edge_b[...] = both[1]


def mid_kernel(other, other_edges, w_qkv, qkv, bias, other_kv, mix):
    tokens = [other[...].astype(F32), other_edges[0].astype(F32), other_edges[1].astype(F32)]
    theirs = mm(jnp.concatenate(tokens, axis=0).astype(BF16), w_qkv[:, D:])
    other_kv[...] = theirs[2 * UNIT :]
    for g in range(2):
        part = slice(g * UNIT, (g + 1) * UNIT)
        keys = jnp.concatenate([qkv[part, D : 2 * D], theirs[part, :D]], axis=0).astype(BF16)
        values = jnp.concatenate([qkv[part, 2 * D :], theirs[part, D:]], axis=0).astype(BF16)
        mix[part, :] = attend(qkv[part, :D], keys, values, bias[g])


def erf_gelu(v):
    return v * (1.0 + lax.erf(v * math.sqrt(0.5))) * 0.5


def last_kernel(near_a, far_a, near_b, far_b, w_qkv, qkv, other_kv, bias, mid, w_out, start, to_final, mlp_gain,
                w_up, w_down, out):
    parts = [mid[...]]
    upper = lax.broadcasted_iota(jnp.int32, (2 * HALF - UNIT, D), 0) < UNIT // 2 - HALVES[1][0]
    halos = [halo[...].astype(F32) for halo in (near_a, far_a, near_b, far_b)]
    halo_kv = mm(jnp.concatenate(halos, axis=0).astype(BF16), w_qkv[:, D:])
    for e in range(2):
        own = slice((2 + e) * UNIT, (3 + e) * UNIT)
        theirs = slice(e * UNIT, (e + 1) * UNIT)
        pieces = [qkv[own, D:], other_kv[theirs, :]]
        pieces += [halo_kv[(2 * e + i) * UNIT : (2 * e + i + 1) * UNIT] for i in range(2)]
        queries = qkv[own, :D]
        done = []
        for g, (low, high) in enumerate(HALVES):
            keys = jnp.concatenate([p[low:high, :D] for p in pieces], axis=0).astype(BF16)
            values = jnp.concatenate([p[low:high, D:] for p in pieces], axis=0).astype(BF16)
            done.append(attend(queries[low:high], keys, values, bias[e, g]))
        cut = HALVES[1][0]
        shared = jnp.where(upper, done[0][cut:], done[1][: HALF - cut])
        parts += [done[0][:cut], shared, done[1][HALF - cut :]]
    mix = jnp.concatenate(parts, axis=0).astype(BF16)
    mix = mm(to_final[...], mix).astype(BF16)
    attended = start[...] + mm(mix, w_out[...])
    mlp_in = norm(attended, mlp_gain[...]).astype(BF16)
    total = attended
    width = w_up.shape[1]
    step = 2048
    for c in range(0, width, step):
        hidden = erf_gelu(mm(mlp_in, w_up[:, c : c + step])).astype(BF16)
        total = total + mm(hidden, w_down[c : c + step, :])
    for b in range(SH):
        for j in range(SW):
            at = (b * SW + j) * LATENT
            out[b, j] = total[at : at + LATENT]


def call(kernel, outs, *args, smem=(), hbm=(), hbm_out=(), scratch=(), limit=24, flops=10**9):
    specs = []
    for i in range(len(args)):
        space = pltpu.SMEM if i in smem else pltpu.HBM if i in hbm else pltpu.VMEM
        specs.append(pl.BlockSpec(memory_space=space))
    out_specs = [
        pl.BlockSpec(memory_space=pltpu.HBM if i in hbm_out else pltpu.VMEM) for i in range(len(outs))
    ]
    moved = sum(a.size * a.dtype.itemsize for a in args)
    return pl.pallas_call(
        kernel,
        out_shape=[jax.ShapeDtypeStruct(s, d) for s, d in outs],
        in_specs=specs,
        out_specs=out_specs,
        scratch_shapes=list(scratch),
        compiler_params=pltpu.CompilerParams(vmem_limit_bytes=limit << 20),
        cost_estimate=pl.CostEstimate(flops=flops, bytes_accessed=moved, transcendentals=0),
    )(*args)


def swap_pairs(change, turn=0):
    pairs = []
    for l in range(LEVELS):
        for a in range(4):
            for o in range(4):
                target = change(a, o)
                if target is not None:
                    level = l ^ turn if target == (a, o) else l
                    pairs.append(((l * 4 + a) * 4 + o, (level * 4 + target[0]) * 4 + target[1]))
    return pairs


def swap(block, pairs):
    return lax.ppermute(block, MESH_AXES, pairs)


def shards(patches, level_embed, embed_weight, block_ids, latent_queries, cross_gain, cross_query,
           cross_kv, cross_out, region_ids, swin_gain, swin_qkv, swin_out, mlp_gain, mlp_up, mlp_down):
    across = swap_pairs(lambda a, o: (a ^ 1, o))
    first = swap_pairs(lambda a, o: (a, o ^ 1))
    second = swap_pairs(lambda a, o: (a, 3 - o) if o in (1, 2) else None)
    second_all = swap_pairs(lambda a, o: (a, 3 - o) if o in (1, 2) else (a, o), turn=1)
    odd = lax.axis_index("lon") % 2
    features = patches.shape[-1]

    flat = patches[0].transpose(1, 2, 0, 3).reshape(SH * SW * LEVELS, features)
    ids = block_ids.transpose(0, 2, 4, 3, 1).reshape(CAP, 1, LEVELS)
    (packed,) = call(
        embed_kernel, [((LEVELS, SENT, 128), BF16)], ids, flat, embed_weight, level_embed,
        hbm=(0, 1, 2, 3), hbm_out=(0,), limit=63,
        scratch=[
            pltpu.VMEM((SH * SW * LEVELS, features), BF16),
            pltpu.VMEM((features, D), BF16),
            pltpu.VMEM((1, D), F32),
            pltpu.VMEM((D // 128, SH * SW * LEVELS, 128), F32),
            pltpu.VMEM((LEVELS, SENT, 128), BF16),
            pltpu.SMEM((CAP, 1, LEVELS), jnp.int32),
            pltpu.SemaphoreType.DMA((SH + 3 + LEVELS,)),
        ],
    )
    packed, region_ids, odd = lax.optimization_barrier((packed, region_ids, odd))
    received = lax.all_to_all(packed, "lvl", 0, 0, tiled=True)

    labels = jnp.pad(region_ids.astype(F32) + 1.0, ((0, 2), (0, 116)))
    other_labels = swap(labels, across)
    both = jnp.stack([labels, other_labels])
    far_labels_a, far_labels_b = swap(both, first), swap(both, second)
    rows, cols, spans = label_pickers()
    odd_one = odd.astype(jnp.int32).reshape(1)
    mid_bias, edge_bias = call(
        prep_kernel, [((2, UNIT, 2 * UNIT), F32), ((2, 2, HALF, 4 * HALF), F32)],
        labels, other_labels, far_labels_a, far_labels_b, rows, cols, spans, odd_one, smem=(7,),
    )
    to_unit_even, to_final_even = permutations(SW - EDGE)
    to_unit_odd, to_final_odd = permutations(0)
    to_unit = jnp.where(odd == 1, to_unit_odd, to_unit_even).astype(BF16)
    to_final = jnp.where(odd == 1, to_final_odd, to_final_even).astype(BF16)
    to_last = jnp.asarray(final_permutation(), BF16)

    received, mid_bias, edge_bias = lax.optimization_barrier((received, mid_bias, edge_bias))
    normed, edges, edge_a, edge_b, mixed = call(
        cross_kernel,
        [((TOKENS, D), BF16), ((2, UNIT, D), BF16)] + [((UNIT, D), BF16)] * 2 + [((TOKENS, D), BF16)],
        received, cross_gain[None], cross_query, cross_kv, latent_queries, cross_out, swin_gain[None],
        to_unit, hbm_out=(4,), flops=4 * 10**9,
        scratch=[pltpu.VMEM((TOKENS, D), BF16), pltpu.SemaphoreType.DMA],
    )
    other_edges = swap(edges, across)
    near_a, near_b = swap(edge_a, first), swap(edge_b, second_all)
    qkv, start, centre = call(
        own_kernel, [((TOKENS, 3 * D), F32), ((TOKENS, D), F32), ((2 * UNIT, D), BF16)],
        normed, mixed, swin_qkv, cross_out, latent_queries, to_last, mlp_up, mlp_down, flops=3 * 10**9,
    )
    other_centre = swap(centre, across)
    other_a, other_b = call(split_kernel, [((UNIT, D), BF16)] * 2, other_edges)
    far_a, far_b = swap(other_a, first), swap(other_b, second_all)
    other_kv, mid = call(
        mid_kernel, [((2 * UNIT, 2 * D), F32), ((2 * UNIT, D), F32)], other_centre, other_edges, swin_qkv, qkv, mid_bias,
        flops=3 * 10**9,
    )
    (out,) = call(
        last_kernel, [((SH, SW, LATENT, D), F32)],
        near_a, far_a, near_b, far_b, swin_qkv, qkv, other_kv, edge_bias, mid, swin_out, start, to_final,
        mlp_gain[None], mlp_up, mlp_down, flops=8 * 10**9,
    )
    return out.transpose(2, 0, 1, 3)


def solution(mesh):
    return jax.shard_map(
        shards,
        mesh=mesh,
        in_specs=(
            P("lvl", None, "lat", "lon", None), P("lvl", None), P(), P("lvl", None, "lat", "lon", None),
            P(), P(), P(), P(), P(), P(("lvl", "lat"), "lon"), P(), P(), P(), P(), P(), P(),
        ),
        out_specs=P(None, ("lvl", "lat"), "lon", None),
        check_vma=False,
    )
```

```python
import functools
import math

import jax
import jax.numpy as jnp
import numpy as np
from jax import lax
from jax.experimental import pallas as pl
from jax.experimental.pallas import tpu as pltpu
from jax.sharding import PartitionSpec as P

D = 512
HEADS = 16
HEAD = D // HEADS
ROOT = 1.0 / math.sqrt(HEAD)
LEVELS = 16
LATENT = 4
CAP = 3
SH = 6
SW = 12
EDGE = 3
CELLS = SH * SW
UNIT = 72
HALF = 40
HALVES = ((0, HALF), (UNIT - HALF, UNIT))
TOKENS = LATENT * CELLS
SLOT_ROWS = CAP * SW
MAIN = 32
REST = SLOT_ROWS - MAIN
GROUPS = D // 128
SENT = GROUPS * SLOT_ROWS + 8
RECV = LEVELS * SLOT_ROWS
MESH_AXES = ("lvl", "lat", "lon")
NEG = -1e30
F32 = jnp.float32
BF16 = jnp.bfloat16


def unit_tokens(first_edge):
    order = []
    for levels in ((0, 3), (1, 2)):
        order += [(p, b, EDGE + j) for p in levels for b in range(SH) for j in range(2 * EDGE)]
    for start in (first_edge, SW - EDGE - first_edge):
        order += [(p, b, start + j) for p in (0, 3, 1, 2) for b in range(SH) for j in range(EDGE)]
    return order


def permutations(first_edge):
    to_unit = np.zeros((TOKENS, TOKENS), np.float32)
    to_final = np.zeros((TOKENS, TOKENS), np.float32)
    for t, (p, b, j) in enumerate(unit_tokens(first_edge)):
        cell = b * SW + j
        to_unit[t, p * CELLS + cell] = 1
        to_final[cell * LATENT + p, t] = 1
    return to_unit, to_final


def final_permutation():
    out = np.zeros((TOKENS, TOKENS), np.float32)
    for cell in range(CELLS):
        for p in range(LATENT):
            out[cell * LATENT + p, p * CELLS + cell] = 1
    return out


def label_pickers():
    rows = np.zeros((3, 128, 128), np.float32)
    cols = np.zeros((2, 8, 128), np.float32)
    spans = np.zeros((8, 128), np.float32)
    tokens = unit_tokens(0)
    window = [(p + 1) // 2 for p in range(LATENT)]
    for i in range(UNIT):
        _, b, j = tokens[i]
        rows[0, j, i] = 1
        cols[0, b, i] = 1
        for u in range(3):
            spans[u, i] = 4 * window[tokens[u * UNIT + i][0]]
        _, b, j = tokens[2 * UNIT + i]
        rows[1, j, i] = 1
        rows[2, j + SW - EDGE, i] = 1
        cols[1, b, i] = 1
    return rows, cols, spans


def nt(a, b):
    return lax.dot_general(a, b, (((1,), (1,)), ((), ())), preferred_element_type=F32)


def mm(a, b):
    return jnp.dot(a, b, preferred_element_type=F32)


def norm(x, gain):
    mean = jnp.mean(x, axis=-1, keepdims=True)
    centred = x - mean
    var = jnp.mean(centred * centred, axis=-1, keepdims=True)
    return centred * lax.rsqrt(var + 1e-05) * gain


def head_rows():
    lane = lax.broadcasted_iota(jnp.int32, (HEADS, D), 1) // HEAD
    head = lax.broadcasted_iota(jnp.int32, (HEADS, D), 0)
    return jnp.where(lane == head, 1.0, 0.0).astype(F32)


def embed_kernel(ids_hbm, patches_hbm, weight_hbm, level_hbm, out_hbm, patches, weight, level, emb,
                 packed, ids, sems):
    copy_ids = pltpu.make_async_copy(ids_hbm, ids, sems.at[SH + 2 + LEVELS])
    copy_ids.start()
    copy_w = pltpu.make_async_copy(weight_hbm, weight, sems.at[SH])
    copy_w.start()
    rows = SW * LEVELS
    copies = []
    for b in range(SH):
        part = pl.ds(b * rows, rows)
        copy = pltpu.make_async_copy(patches_hbm.at[part], patches.at[part], sems.at[b])
        copy.start()
        copies.append(copy)
    copy_level = pltpu.make_async_copy(level_hbm, level, sems.at[SH + 1])
    copy_level.start()
    copy_w.wait()
    for b in range(0, SH, 3):
        for k in range(b, b + 3):
            copies[k].wait()
        part = pl.ds(b * rows, 3 * rows)
        block = mm(patches[part, :], weight[...])
        for g in range(D // 128):
            emb[g, part, :] = block[:, g * 128 : (g + 1) * 128]
    copy_level.wait()
    copy_ids.wait()
    shift = level[...]
    sub = lax.broadcasted_iota(jnp.int32, (8, 128), 0)
    sends = []
    for m in range(LEVELS):
        tail = jnp.full(sub.shape, -1.0, F32)
        parts = []
        for s in range(CAP):
            slot = ids[s, 0, m]
            start = jnp.maximum(slot, 0) * rows + m
            picked = [emb[g, pl.ds(start, SW, stride=LEVELS), :] for g in range(D // 128)]
            parts.append(jnp.concatenate(picked, axis=1) + shift)
            tail = jnp.where(sub == s, slot.astype(F32), tail)
        rows_m = jnp.concatenate(parts, axis=0)
        groups = [rows_m[:, g * 128 : (g + 1) * 128] for g in range(GROUPS)]
        order = [v[:MAIN] for v in groups] + [v[MAIN:] for v in groups] + [tail]
        packed[m] = jnp.concatenate(order, axis=0).astype(BF16)
        send = pltpu.make_async_copy(packed.at[m], out_hbm.at[m], sems.at[SH + 2 + m])
        send.start()
        sends.append(send)
    for send in sends:
        send.wait()


def prep_kernel(own, other, far_a, far_b, pick_rows, pick_cols, spans, odd, mid_bias, edge_bias):
    is_odd = odd[0] == 1
    high_first = jnp.where(is_odd, 1, 2)
    row_a = pick_rows[high_first]
    row_b = pick_rows[3 - high_first]

    def codes(labels, row_pick, which, span):
        spread = mm(labels, row_pick) * pick_cols[which]
        return jnp.sum(spread, axis=0, keepdims=True) + spans[span : span + 1, :]

    def column(row):
        return jnp.broadcast_to(row, (8, 128)).T[:UNIT, :1]

    def bias(query, keys):
        return jnp.concatenate(
            [jnp.where(column(query) == k[:, :UNIT], 0.0, NEG) for k in keys], axis=1
        )

    for g in range(2):
        mine = codes(own[...], pick_rows[0], 0, g)
        theirs = codes(other[...], pick_rows[0], 0, g)
        mid_bias[g] = bias(mine, [mine, theirs])
    for e, (near, away, far) in enumerate(((row_a, row_b, far_a), (row_b, row_a, far_b))):
        mine = codes(own[...], near, 1, 2)
        theirs = codes(other[...], near, 1, 2)
        halo = codes(far[0], away, 1, 2)
        halo_other = codes(far[1], away, 1, 2)
        for g, (low, high) in enumerate(HALVES):
            parts = [k[:, low:high] for k in (mine, theirs, halo, halo_other)]
            keys = jnp.concatenate(parts, axis=1)
            edge_bias[e, g] = jnp.where(column(mine)[low:high] == keys, 0.0, NEG)


def cross_kernel(recv, gain, wq, w_kv, lq, w_out, swin_gain, to_unit, normed, edges,
                 edge_a, edge_b, mixed_hbm, mixed, sem):
    queries = (mm(lq[...], wq[...]) * ROOT).astype(BF16).astype(F32)
    mask = head_rows()
    masked = jnp.concatenate([queries[q : q + 1, :] * mask for q in range(LATENT)], axis=0)
    wkq = nt(w_kv[:, :D], masked.astype(BF16)).astype(BF16)
    main, rest, lists = [], [], []
    for l in range(LEVELS):
        tile = recv[l].astype(F32)
        main.append(
            jnp.concatenate([tile[g * MAIN : (g + 1) * MAIN] for g in range(GROUPS)], axis=1)
        )
        tail = tile[GROUPS * MAIN : GROUPS * SLOT_ROWS]
        rest.append(
            jnp.concatenate([tail[g * REST : (g + 1) * REST] for g in range(GROUPS)], axis=1)
        )
        lists.append(tile[GROUPS * SLOT_ROWS :])
    x = jnp.concatenate(main + rest, axis=0)
    keys_in = norm(x, gain[...]).astype(BF16)
    values = mm(keys_in, w_kv[:, D:]).astype(BF16).astype(F32)
    scores = mm(keys_in, wkq)
    row = lax.broadcasted_iota(jnp.int32, (MAIN, 128), 0)
    slot = jnp.where(row >= 2 * SW, 2, jnp.where(row >= SW, 1, 0))
    place = (row - slot * SW).astype(F32)
    tail_row = lax.broadcasted_iota(jnp.int32, (2 * REST, 128), 0)
    tail_place = (jnp.where(tail_row < REST, tail_row, tail_row - REST) + (SW - REST)).astype(F32)
    tags = []
    for ids in lists:
        block = jnp.where(slot == 0, ids[0:1], jnp.where(slot == 1, ids[1:2], ids[2:3]))
        tags.append(jnp.where(block >= 0, block * SW + place, -1.0))
    for l in range(0, LEVELS, 2):
        block = jnp.where(tail_row < REST, lists[l][2:3], lists[l + 1][2:3])
        tags.append(jnp.where(block >= 0, block * SW + tail_place, -1.0))
    tag = jnp.concatenate(tags, axis=0)
    lane = lax.broadcasted_iota(jnp.int32, (RECV, 128), 1).astype(F32)
    hit = jnp.where(tag == lane, 1.0, 0.0)
    hit_t = hit.T[:CELLS].astype(BF16)
    hit = hit.astype(BF16)
    present = tag[:, :64] >= 0
    weight = jnp.where(present, jnp.exp(scores), 0.0)

    def halves(v):
        high = v.astype(BF16)
        return jnp.concatenate([high.astype(F32), v - high.astype(F32)], axis=1).astype(BF16)

    total = mm(hit_t, halves(weight))
    total = total[:, :64] + total[:, 64:]
    spread = mm(hit[:, :CELLS], halves(total))
    spread = spread[:, :64] + spread[:, 64:]
    weight = (weight / jnp.where(present, spread, 1.0)).astype(BF16)
    values = values.astype(BF16)
    rows = []
    for q in range(LATENT):
        rows.append(jnp.concatenate([mask if k == q else jnp.zeros_like(mask) for k in range(LATENT)], axis=1))
    wide = mm(weight, jnp.concatenate(rows, axis=0).astype(BF16)).astype(BF16)
    sums = mm(hit_t, wide * jnp.concatenate([values] * LATENT, axis=1))
    starts = [sums[:, q * D : (q + 1) * D] for q in range(LATENT)]
    mix = jnp.concatenate(starts, axis=0).astype(BF16)
    mixed[...] = mix
    keep = pltpu.make_async_copy(mixed, mixed_hbm, sem)
    keep.start()
    projected = mm(mix, w_out[...])
    queries = lq[...].astype(F32)
    start = jnp.concatenate(
        [projected[q * CELLS : (q + 1) * CELLS] + queries[q : q + 1] for q in range(LATENT)], axis=0
    )
    unit = norm(start, swin_gain[...]).astype(BF16)
    placed = mm(to_unit[...], unit)
    normed[...] = placed.astype(BF16)
    for e, edge in enumerate((edge_a, edge_b)):
        tokens = placed[(2 + e) * UNIT : (3 + e) * UNIT].astype(BF16)
        edges[e] = tokens
        edge[...] = tokens
    keep.wait()


def own_kernel(normed, mixed, w_qkv, w_out, lq, to_last, w_up, w_down, qkv, start, centre):
    centre[...] = normed[: 2 * UNIT, :]
    proj = mm(normed[...], w_qkv[...])
    qkv[:, :D] = proj[:, :D] * ROOT
    qkv[:, D:] = proj[:, D:]
    last = mm(to_last[...], mixed[...]).astype(BF16)
    level = lax.broadcasted_iota(jnp.int32, (TOKENS, D), 0) % LATENT
    queries = lq[...].astype(F32)
    rows = jnp.broadcast_to(queries[LATENT - 1 :], (TOKENS, D))
    for p in range(LATENT - 1):
        rows = jnp.where(level == p, queries[p : p + 1], rows)
    start[...] = mm(last, w_out[...]) + rows


def attend(queries, keys, values, bias):
    rows = queries.shape[0]
    lane = lax.broadcasted_iota(jnp.int32, (rows, 128), 1) // HEAD
    masks = [jnp.where(lane == h, 1.0, 0.0) for h in range(4)]
    outs = []
    tall = jnp.concatenate([bias] * 4, axis=0)
    for g in range(4):
        cols = slice(g * 128, (g + 1) * 128)
        stack = jnp.concatenate([jnp.where(lane == h, queries[:, cols], 0.0) for h in range(4)], axis=0).astype(BF16)
        scores = nt(stack, keys[:, cols]) + tall
        top = jnp.max(scores, axis=-1, keepdims=True)
        exps = jnp.exp(scores - top)
        total = jnp.sum(exps, axis=-1, keepdims=True)
        part = mm(exps.astype(BF16), values[:, cols])
        out, scale = part[:rows], jnp.broadcast_to(total[:rows], (rows, 128))
        for h in range(1, 4):
            here = slice(h * rows, (h + 1) * rows)
            out = jnp.where(lane == h, part[here], out)
            scale = jnp.where(lane == h, total[here], scale)
        outs.append(out / scale)
    return jnp.concatenate(outs, axis=1)


def split_kernel(both, edge_a, edge_b):
    edge_a[...] = both[0]
    edge_b[...] = both[1]


def mid_kernel(other, other_edges, w_qkv, qkv, bias, other_kv, mix):
    tokens = [other[...].astype(F32), other_edges[0].astype(F32), other_edges[1].astype(F32)]
    theirs = mm(jnp.concatenate(tokens, axis=0).astype(BF16), w_qkv[:, D:])
    other_kv[...] = theirs[2 * UNIT :]
    for g in range(2):
        part = slice(g * UNIT, (g + 1) * UNIT)
        keys = jnp.concatenate([qkv[part, D : 2 * D], theirs[part, :D]], axis=0).astype(BF16)
        values = jnp.concatenate([qkv[part, 2 * D :], theirs[part, D:]], axis=0).astype(BF16)
        mix[part, :] = attend(qkv[part, :D], keys, values, bias[g])


def erf_gelu(v):
    return v * (1.0 + lax.erf(v * math.sqrt(0.5))) * 0.5


def last_kernel(near_a, far_a, near_b, far_b, w_qkv, qkv, other_kv, bias, mid, w_out, start, to_final, mlp_gain,
                w_up, w_down, out):
    parts = [mid[...]]
    upper = lax.broadcasted_iota(jnp.int32, (2 * HALF - UNIT, D), 0) < UNIT // 2 - HALVES[1][0]
    halos = [halo[...].astype(F32) for halo in (near_a, far_a, near_b, far_b)]
    halo_kv = mm(jnp.concatenate(halos, axis=0).astype(BF16), w_qkv[:, D:])
    for e in range(2):
        own = slice((2 + e) * UNIT, (3 + e) * UNIT)
        theirs = slice(e * UNIT, (e + 1) * UNIT)
        pieces = [qkv[own, D:], other_kv[theirs, :]]
        pieces += [halo_kv[(2 * e + i) * UNIT : (2 * e + i + 1) * UNIT] for i in range(2)]
        queries = qkv[own, :D]
        done = []
        for g, (low, high) in enumerate(HALVES):
            keys = jnp.concatenate([p[low:high, :D] for p in pieces], axis=0).astype(BF16)
            values = jnp.concatenate([p[low:high, D:] for p in pieces], axis=0).astype(BF16)
            done.append(attend(queries[low:high], keys, values, bias[e, g]))
        cut = HALVES[1][0]
        shared = jnp.where(upper, done[0][cut:], done[1][: HALF - cut])
        parts += [done[0][:cut], shared, done[1][HALF - cut :]]
    mix = jnp.concatenate(parts, axis=0).astype(BF16)
    mix = mm(to_final[...], mix).astype(BF16)
    attended = start[...] + mm(mix, w_out[...])
    mlp_in = norm(attended, mlp_gain[...]).astype(BF16)
    total = attended
    width = w_up.shape[1]
    step = 2048
    for c in range(0, width, step):
        hidden = erf_gelu(mm(mlp_in, w_up[:, c : c + step])).astype(BF16)
        total = total + mm(hidden, w_down[c : c + step, :])
    for b in range(SH):
        for j in range(SW):
            at = (b * SW + j) * LATENT
            out[b, j] = total[at : at + LATENT]


def call(kernel, outs, *args, smem=(), hbm=(), hbm_out=(), scratch=(), limit=24, flops=10**9):
    specs = []
    for i in range(len(args)):
        space = pltpu.SMEM if i in smem else pltpu.HBM if i in hbm else pltpu.VMEM
        specs.append(pl.BlockSpec(memory_space=space))
    out_specs = [
        pl.BlockSpec(memory_space=pltpu.HBM if i in hbm_out else pltpu.VMEM) for i in range(len(outs))
    ]
    moved = sum(a.size * a.dtype.itemsize for a in args)
    return pl.pallas_call(
        kernel,
        out_shape=[jax.ShapeDtypeStruct(s, d) for s, d in outs],
        in_specs=specs,
        out_specs=out_specs,
        scratch_shapes=list(scratch),
        compiler_params=pltpu.CompilerParams(vmem_limit_bytes=limit << 20),
        cost_estimate=pl.CostEstimate(flops=flops, bytes_accessed=moved, transcendentals=0),
    )(*args)


def swap_pairs(change, turn=0):
    pairs = []
    for l in range(LEVELS):
        for a in range(4):
            for o in range(4):
                target = change(a, o)
                if target is not None:
                    level = l ^ turn if target == (a, o) else l
                    pairs.append(((l * 4 + a) * 4 + o, (level * 4 + target[0]) * 4 + target[1]))
    return pairs


def swap(block, pairs):
    return lax.ppermute(block, MESH_AXES, pairs)


def shards(patches, level_embed, embed_weight, block_ids, latent_queries, cross_gain, cross_query,
           cross_kv, cross_out, region_ids, swin_gain, swin_qkv, swin_out, mlp_gain, mlp_up, mlp_down):
    across = swap_pairs(lambda a, o: (a ^ 1, o))
    first = swap_pairs(lambda a, o: (a, o ^ 1))
    second = swap_pairs(lambda a, o: (a, 3 - o) if o in (1, 2) else None)
    second_all = swap_pairs(lambda a, o: (a, 3 - o) if o in (1, 2) else (a, o), turn=1)
    odd = lax.axis_index("lon") % 2
    features = patches.shape[-1]

    flat = patches[0].transpose(1, 2, 0, 3).reshape(SH * SW * LEVELS, features)
    ids = block_ids.transpose(0, 2, 4, 3, 1).reshape(CAP, 1, LEVELS)
    (packed,) = call(
        embed_kernel, [((LEVELS, SENT, 128), BF16)], ids, flat, embed_weight, level_embed,
        hbm=(0, 1, 2, 3), hbm_out=(0,), limit=63,
        scratch=[
            pltpu.VMEM((SH * SW * LEVELS, features), BF16),
            pltpu.VMEM((features, D), BF16),
            pltpu.VMEM((1, D), F32),
            pltpu.VMEM((D // 128, SH * SW * LEVELS, 128), F32),
            pltpu.VMEM((LEVELS, SENT, 128), BF16),
            pltpu.SMEM((CAP, 1, LEVELS), jnp.int32),
            pltpu.SemaphoreType.DMA((SH + 3 + LEVELS,)),
        ],
    )
    packed, region_ids, odd = lax.optimization_barrier((packed, region_ids, odd))
    received = lax.all_to_all(packed, "lvl", 0, 0, tiled=True)

    labels = jnp.pad(region_ids.astype(F32) + 1.0, ((0, 2), (0, 116)))
    other_labels = swap(labels, across)
    both = jnp.stack([labels, other_labels])
    far_labels_a, far_labels_b = swap(both, first), swap(both, second)
    rows, cols, spans = label_pickers()
    odd_one = odd.astype(jnp.int32).reshape(1)
    mid_bias, edge_bias = call(
        prep_kernel, [((2, UNIT, 2 * UNIT), F32), ((2, 2, HALF, 4 * HALF), F32)],
        labels, other_labels, far_labels_a, far_labels_b, rows, cols, spans, odd_one, smem=(7,),
    )
    to_unit_even, to_final_even = permutations(SW - EDGE)
    to_unit_odd, to_final_odd = permutations(0)
    to_unit = jnp.where(odd == 1, to_unit_odd, to_unit_even).astype(BF16)
    to_final = jnp.where(odd == 1, to_final_odd, to_final_even).astype(BF16)
    to_last = jnp.asarray(final_permutation(), BF16)

    received, mid_bias, edge_bias = lax.optimization_barrier((received, mid_bias, edge_bias))
    normed, edges, edge_a, edge_b, mixed = call(
        cross_kernel,
        [((TOKENS, D), BF16), ((2, UNIT, D), BF16)] + [((UNIT, D), BF16)] * 2 + [((TOKENS, D), BF16)],
        received, cross_gain[None], cross_query, cross_kv, latent_queries, cross_out, swin_gain[None],
        to_unit, hbm_out=(4,), flops=4 * 10**9,
        scratch=[pltpu.VMEM((TOKENS, D), BF16), pltpu.SemaphoreType.DMA],
    )
    other_edges = swap(edges, across)
    near_a, near_b = swap(edge_a, first), swap(edge_b, second_all)
    qkv, start, centre = call(
        own_kernel, [((TOKENS, 3 * D), F32), ((TOKENS, D), F32), ((2 * UNIT, D), BF16)],
        normed, mixed, swin_qkv, cross_out, latent_queries, to_last, mlp_up, mlp_down, flops=3 * 10**9,
    )
    other_centre = swap(centre, across)
    other_a, other_b = call(split_kernel, [((UNIT, D), BF16)] * 2, other_edges)
    far_a, far_b = swap(other_a, first), swap(other_b, second_all)
    other_kv, mid = call(
        mid_kernel, [((2 * UNIT, 2 * D), F32), ((2 * UNIT, D), F32)], other_centre, other_edges, swin_qkv, qkv, mid_bias,
        flops=3 * 10**9,
    )
    (out,) = call(
        last_kernel, [((SH, SW, LATENT, D), F32)],
        near_a, far_a, near_b, far_b, swin_qkv, qkv, other_kv, edge_bias, mid, swin_out, start, to_final,
        mlp_gain[None], mlp_up, mlp_down, flops=8 * 10**9,
    )
    return out.transpose(2, 0, 1, 3)


def solution(mesh):
    return jax.shard_map(
        shards,
        mesh=mesh,
        in_specs=(
            P("lvl", None, "lat", "lon", None), P("lvl", None), P(), P("lvl", None, "lat", "lon", None),
            P(), P(), P(), P(), P(), P(("lvl", "lat"), "lon"), P(), P(), P(), P(), P(), P(),
        ),
        out_specs=P(None, ("lvl", "lat"), "lon", None),
        check_vma=False,
    )
```
